32 devices in a mesh: expert: 8 (over z, x), dp: 4 (over y, core).
Axes of the slice: x: 2, y: 2, z: 4, core: 2. Of those that a mesh axis runs over, the one named last changes fastest.
Arguments:
- tokens: bfloat16 [4096, 2048], P(('expert', 'dp')), may hold values from -6 to 6
- out_grad: bfloat16 [4096, 2048], P(('expert', 'dp')), may hold values from -6 to 6
- route_weights: bfloat16 [4096, 8], P(('expert', 'dp')), may hold values from 0.05 to 2.5, as said below
- expert_ids: int32 [4096, 8], P(('expert', 'dp')), may hold values from 0 to 15, all different within a row; in each aligned block of 128 rows (0 to 127, 128 to 255, ...) at most 96 rows name the same one
- gate_weight: bfloat16 [16, 2048, 384], P('expert'), may hold values from -0.125 to 0.125
- up_weight: bfloat16 [16, 2048, 384], P('expert'), may hold values from -0.125 to 0.125
- down_weight: bfloat16 [16, 384, 2048], P('expert'), may hold values from -0.3125 to 0.3125
Outputs:
- grad_input: bfloat16 [4096, 2048], P(('expert', 'dp'))
- grad_gate: bfloat16 [16, 2048, 384], P('expert', 'dp')
- grad_up: bfloat16 [16, 2048, 384], P('expert', 'dp')
- grad_down: bfloat16 [16, 384, 2048], P('expert', 'dp')
- expert_load: float32 [16], replicated
The draws below stay inside these ranges and needn't reach their ends.
Inputs may be any that keep to these rules, and one draw needn't show every extreme that they name: `expert_ids`: each row names 8 different experts. Within each aligned block of 128 rows (the rows of one device) no expert is named by more than 96 rows, a bound that some block reaches. `route_weights`: positive router weights.
All inputs are finite; a program needn't handle non-finite values.
Results may differ from the reference program's by a relative error of at most 0.009.
Values may be sent and summed in bfloat16 or wider, within the bound.
No kernel may reach another device: no remote copies, remote signals or barrier semaphores. Data moves between devices by JAX's collectives and lax.ppermute only.
A program may use at most 192 MiB of HBM per device.

```python
import math
import jax
import jax.numpy as jnp
import numpy as np
from jax import lax

D = 2048
F = 384
TOP = 8
TOK_DEV = 128
EXPERTS = 16
CAP = 96
TOKENS = 4096
N_EXPERT = 8
N_DP = 4


def draw_route_weights(key, part):
    row_share = jnp.arange(TOKENS, dtype=jnp.float32)[:, None] / (TOKENS - 1)
    lowest = jnp.log(0.05)
    highest = jnp.log(0.5)
    base = jnp.exp(jax.random.uniform(key, (TOKENS, TOP), jnp.float32, lowest, highest))
    ramp = 1.0 + 2.0 * row_share
    return (base * ramp).astype(jnp.bfloat16)


def shard_levels(key, shape, shards, least, top_value):
    factor_of = 1.0
    for position, shards_of in shards:
        steps = jax.random.uniform(jax.random.fold_in(jax.random.fold_in(key, 6), position), (shards_of,), jnp.float32, least / len(shards), top_value / len(shards))
        factor_of = factor_of * jnp.repeat(jnp.exp(steps), shape[position] // shards_of).reshape((-1,) + (1,) * (len(shape) - 1 - position))
    return factor_of


def assign_block(key, own, number, rows, number_of, top, reach, skew):
    ranking = jax.random.permutation(key, number_of)
    heavy_load, common = load_shares(number_of, rows * top, reach, skew, True), load_shares(number_of, rows * top, reach, skew, False)
    places = jnp.arange(number_of)

    def named(sizes, offset_by):
        used = int((sizes > 0).sum())
        fixed = max(1, used // 4)
        moved = fixed + (places - fixed + offset_by * (used - fixed)) % max(1, number_of - fixed)
        return jnp.zeros((number_of,), jnp.int32).at[ranking[jnp.where(places < fixed, places, moved)]].set(jnp.asarray(sizes, jnp.int32))

    sizes = jnp.where(number % 4 == 0, named(heavy_load, number // 4), named(common, number - number // 4 - 1))
    mixed = jax.random.permutation(jax.random.fold_in(own, 3), number_of)
    source_of, sink = mixed[0:number_of // 2 * 2:2], mixed[1:number_of // 2 * 2:2]
    room = jnp.minimum(sizes[source_of] - 1, reach - sizes[sink]) // 2
    room = jnp.where((source_of == ranking[0]) | (sink == ranking[0]) | (sizes[sink] == 0), 0, jnp.maximum(room, 0))
    moved = jax.random.randint(jax.random.fold_in(own, 4), (number_of // 2,), 0, 1 << 20) % (room + 1)
    sizes = sizes.at[source_of].add(-moved).at[sink].add(moved)
    labels = jnp.searchsorted(jnp.cumsum(sizes), jnp.arange(rows * top), side="right").astype(jnp.int32)
    listing = labels.reshape(top, rows).T
    listing = listing[jax.random.permutation(jax.random.fold_in(own, 1), rows)]
    offset_by = jax.random.randint(jax.random.fold_in(own, 2), (rows, 1), 0, top)
    return jnp.take_along_axis(listing, (jnp.arange(top)[None, :] + offset_by) % top, axis=1)


def load_shares(count, total, most, slope, full):
    weights = [(1 << 20) // math.isqrt(grade ** slope) + 1 for grade in range(1, count + 1)]
    largest = most if full else min(most, max(-(-total // count), total * weights[0] // sum(weights)))
    least = 1 if total - largest >= count - 1 else 0
    holding, rest = [largest] + [least] * (count - 1), total - largest - least * (count - 1)
    while rest > 0:
        free = [i for i in range(1, count) if holding[i] < largest] or [i for i in range(1, count) if holding[i] < most]
        mass, left = sum([weights[i] for i in free]), rest
        for i in free:
            addition = min(most - holding[i], max(1, left * weights[i] // mass), rest)
            holding[i] = holding[i] + addition
            rest = rest - addition
    return np.array(holding)


def normal_values(rng, shape, scale, bound, cuts=(), kind=jnp.bfloat16):
    loudness = shard_levels(rng, shape, cuts, -0.22, 0.18) if cuts else 1.0
    array = jax.random.normal(rng, shape, jnp.float32) * scale * loudness
    return jnp.minimum(jnp.maximum(array, -bound), bound).astype(kind)


def setup_inputs(seed: int = 0) -> dict:
    streams_of = jax.random.split(jax.random.key(seed), 8)
    tokens = normal_values(streams_of[0], (TOKENS, D), 1.0, 6.0, ((0, 32),))
    out_grad = normal_values(streams_of[1], (TOKENS, D), 1.0, 6.0, ((0, 32),))
    route_weights = draw_route_weights(jax.random.fold_in(streams_of[7], 71), 0)
    expert_ids_keys = jax.random.split(jax.random.fold_in(streams_of[3], 1), TOKENS // TOK_DEV)
    expert_ids_turns = jax.random.permutation(jax.random.fold_in(streams_of[3], 3), TOKENS // TOK_DEV)
    expert_ids = jax.vmap(lambda own, number: assign_block(jax.random.fold_in(streams_of[3], 2), own, number, TOK_DEV, EXPERTS, TOP, CAP, 2))(expert_ids_keys, expert_ids_turns).reshape((TOKENS, TOP))
    gate_weight = normal_values(streams_of[4], (EXPERTS, D, F), D ** -0.5, 0.125, ((0, 8),))
    up_weight = normal_values(streams_of[5], (EXPERTS, D, F), D ** -0.5, 0.125, ((0, 8),))
    down_weight = normal_values(streams_of[6], (EXPERTS, F, D), F ** -0.5, 0.3125, ((0, 8),))
    return dict(tokens=tokens, out_grad=out_grad, route_weights=route_weights, expert_ids=expert_ids, gate_weight=gate_weight, up_weight=up_weight, down_weight=down_weight)


def swiglu_grads(token_rows, grad_rows, route_rows, gate_matrix, up_matrix, down_matrix):
    contract_last = (((1,), (1,)), ((), ()))
    contract_first = (((0,), (0,)), ((), ()))
    gate_linear = jnp.dot(token_rows, gate_matrix, preferred_element_type=jnp.float32)
    up_linear = jnp.dot(token_rows, up_matrix, preferred_element_type=jnp.float32)
    logistic = jax.nn.sigmoid(gate_linear)
    activated = gate_linear * logistic
    hidden = (activated * up_linear).astype(jnp.bfloat16)
    scaled = (route_rows.astype(jnp.float32)[:, None] * grad_rows.astype(jnp.float32)).astype(jnp.bfloat16)
    delta_hidden = lax.dot_general(scaled, down_matrix, contract_last, preferred_element_type=jnp.float32)
    delta_gate = (delta_hidden * up_linear * logistic * (1.0 + gate_linear * (1.0 - logistic))).astype(jnp.bfloat16)
    delta_up = (delta_hidden * activated).astype(jnp.bfloat16)
    pair_grad = lax.dot_general(delta_gate, gate_matrix, contract_last, preferred_element_type=jnp.float32)
    pair_grad = pair_grad + lax.dot_general(delta_up, up_matrix, contract_last, preferred_element_type=jnp.float32)
    gate_part = lax.dot_general(token_rows, delta_gate, contract_first, preferred_element_type=jnp.float32)
    up_part = lax.dot_general(token_rows, delta_up, contract_first, preferred_element_type=jnp.float32)
    down_part = lax.dot_general(hidden, scaled, contract_first, preferred_element_type=jnp.float32)
    return pair_grad, gate_part, up_part, down_part


def reference(tokens, out_grad, route_weights, expert_ids, gate_weight, up_weight, down_weight):
    num_experts = gate_weight.shape[0]
    blocks = N_EXPERT * N_DP
    token_total = tokens.shape[0]
    block_ids = expert_ids.reshape(blocks, TOK_DEV, TOP).astype(jnp.int32)
    expert_iota = jnp.arange(num_experts, dtype=jnp.int32)
    per_token = jnp.sum((block_ids[..., None] == expert_iota).astype(jnp.int32), axis=2)
    route_blocks = route_weights.reshape(blocks, TOK_DEV, TOP).astype(jnp.float32)
    expert_weight = jnp.sum(jnp.where(block_ids[..., None] == expert_iota, route_blocks[..., None], jnp.zeros((), jnp.float32)), axis=(0, 1, 2))
    expert_load = expert_weight * (num_experts / (token_total * TOP))
    earlier = jnp.cumsum(per_token, axis=1) - per_token
    rank_in_block = jnp.take_along_axis(earlier, block_ids, axis=2).astype(jnp.int32)
    block_iota = jnp.arange(blocks, dtype=jnp.int32)[:, None, None]
    token_iota = block_iota * TOK_DEV + jnp.arange(TOK_DEV, dtype=jnp.int32)[None, :, None] + jnp.zeros_like(block_ids)
    slot_place = ((block_ids * blocks + block_iota) * CAP + rank_in_block).reshape(-1).astype(jnp.int32)
    slot_table = jnp.full((num_experts * blocks * CAP,), token_total, jnp.int32)
    slot_table = slot_table.at[slot_place].set(token_iota.reshape(-1).astype(jnp.int32))
    weight_table = jnp.zeros((num_experts * blocks * CAP,), jnp.float32)
    weight_table = weight_table.at[slot_place].set(route_weights.reshape(-1).astype(jnp.float32))
    slot_table = slot_table.reshape(num_experts, N_EXPERT, N_DP, CAP).transpose(0, 2, 1, 3).reshape(num_experts, N_DP, N_EXPERT * CAP)
    weight_table = weight_table.reshape(num_experts, N_EXPERT, N_DP, CAP).transpose(0, 2, 1, 3).reshape(num_experts, N_DP, N_EXPERT * CAP)
    padded_tokens = jnp.concatenate([tokens, jnp.zeros((1, D), tokens.dtype)], axis=0)
    padded_grads = jnp.concatenate([out_grad, jnp.zeros((1, D), out_grad.dtype)], axis=0)
    half_cols = (N_EXPERT // 2) * CAP

    def per_expert(total_dx, scan_items):
        row_table, route_table, gate_matrix, up_matrix, down_matrix = scan_items
        gate_sum = jnp.zeros((D, F), jnp.float32)
        up_sum = jnp.zeros((D, F), jnp.float32)
        down_sum = jnp.zeros((F, D), jnp.float32)
        for group_id in range(N_DP):
            group_gate = jnp.zeros((D, F), jnp.float32)
            group_up = jnp.zeros((D, F), jnp.float32)
            group_down = jnp.zeros((F, D), jnp.float32)
            for lower, upper in ((0, half_cols), (half_cols, N_EXPERT * CAP)):
                row_index = row_table[group_id][lower:upper]
                pair_grad, gate_part, up_part, down_part = swiglu_grads(
                    padded_tokens[row_index], padded_grads[row_index],
                    route_table[group_id][lower:upper].astype(jnp.bfloat16), gate_matrix, up_matrix, down_matrix)
                rounded = lax.optimization_barrier(pair_grad.astype(jnp.bfloat16))
                total_dx = total_dx.at[row_index].add(rounded.astype(jnp.float32), mode="drop")
                gate_kept = lax.optimization_barrier(gate_part.astype(jnp.bfloat16))
                up_kept = lax.optimization_barrier(up_part.astype(jnp.bfloat16))
                down_kept = lax.optimization_barrier(down_part.astype(jnp.bfloat16))
                group_gate = group_gate + gate_kept.astype(jnp.float32)
                group_up = group_up + up_kept.astype(jnp.float32)
                group_down = group_down + down_kept.astype(jnp.float32)
            gate_round = lax.optimization_barrier(group_gate.astype(jnp.bfloat16))
            up_round = lax.optimization_barrier(group_up.astype(jnp.bfloat16))
            down_round = lax.optimization_barrier(group_down.astype(jnp.bfloat16))
            gate_sum = gate_sum + gate_round.astype(jnp.float32)
            up_sum = up_sum + up_round.astype(jnp.float32)
            down_sum = down_sum + down_round.astype(jnp.float32)
        factor = 1.0 / N_DP
        return total_dx, ((gate_sum * factor).astype(jnp.bfloat16), (up_sum * factor).astype(jnp.bfloat16), (down_sum * factor).astype(jnp.bfloat16))

    start_dx = jnp.zeros((token_total, D), jnp.float32)
    total_dx, grad_stack = lax.scan(per_expert, start_dx, (slot_table, weight_table, gate_weight, up_weight, down_weight))
    grad_input = total_dx.astype(jnp.bfloat16)
    return grad_input, grad_stack[0], grad_stack[1], grad_stack[2], expert_load
```

```python
import jax
import jax.numpy as jnp
from jax import lax
from jax.sharding import PartitionSpec as P

BF = jnp.bfloat16
F32 = jnp.float32
LANES = 128


def dot(a, b, ca, cb):
    return lax.dot_general(a, b, (((ca,), (cb,)), ((), ())), preferred_element_type=F32)


def tie(*values):
    return lax.optimization_barrier(values)


def shards(tokens, out_grad, route_weights, expert_ids, gate_weight, up_weight, down_weight):
    local_experts, width, hidden = gate_weight.shape
    devices = lax.axis_size("expert")
    groups = lax.axis_size("dp")
    num_experts = local_experts * devices
    rows, top_count = expert_ids.shape
    outer = devices // 2
    inner_width = local_experts * hidden
    me = lax.axis_index("expert")
    my_group = lax.axis_index("dp")

    def ring(value, step):
        pairs = [(2 * z + x, 2 * ((z + step) % outer) + x) for z in range(outer) for x in range(2)]
        return lax.ppermute(value, "expert", pairs)

    def cross(value):
        return lax.ppermute(value, "expert", [(i, i ^ 1) for i in range(devices)])

    def swap(value, bit):
        return lax.ppermute(value, "dp", [(i, i ^ bit) for i in range(groups)])

    lanes = jnp.arange(LANES, dtype=jnp.int32)
    dense = jnp.sum(
        jnp.where(
            expert_ids[:, :, None] == lanes, route_weights.astype(F32)[:, :, None], 0.0
        ),
        axis=1,
    ).astype(BF)
    grads = jnp.concatenate([out_grad, dense], axis=1)

    gate_up = jnp.concatenate(
        [gate_weight[e] for e in range(local_experts)] + [up_weight[e] for e in range(local_experts)],
        axis=1,
    )
    down = down_weight.reshape(inner_width, width)

    def forward(token_rows):
        linear = dot(token_rows, gate_up, 1, 0)
        return linear

    def backward(linear, grad_rows):
        cotangent = grad_rows[:, :width]
        routes = grad_rows[:, width:].astype(F32)
        weight = jnp.concatenate(
            [
                jnp.broadcast_to(
                    jnp.sum(
                        jnp.where(lanes == me * local_experts + e, routes, 0.0), axis=1, keepdims=True
                    ),
                    (grad_rows.shape[0], hidden),
                )
                for e in range(local_experts)
            ],
            axis=1,
        )
        gate_linear = linear[:, :inner_width]
        up_linear = linear[:, inner_width:]
        delta_hidden = weight * dot(cotangent, down, 1, 1)
        logistic = jax.nn.sigmoid(gate_linear)
        activated = gate_linear * logistic
        scaled_hidden = (weight * activated * up_linear).astype(BF)
        delta_gate = delta_hidden * up_linear * logistic * (1.0 + gate_linear * (1.0 - logistic))
        delta_up = delta_hidden * activated
        delta = jnp.concatenate([delta_gate.astype(BF), delta_up.astype(BF)], axis=1)
        partial = dot(delta, gate_up, 1, 1).astype(BF)
        return partial, delta, scaled_hidden, cotangent

    token_now, grad_now = tokens, grads
    token_cross, grad_cross = None, None
    first_grad_cross = None
    results = []
    flying_a = (ring(token_now, 1), cross(token_now))
    flying_b = (ring(grad_now, 1), cross(grad_now))
    held = ()
    for step in range(outer + 1):
        token_rows = [t for t in (token_now, token_cross) if t is not None]
        token_block = token_rows[0] if len(token_rows) == 1 else jnp.concatenate(token_rows, axis=0)
        linear = forward(token_block)
        if step > 0:
            got = tie(*flying_b, linear)
            linear = got[-1]
            if step < outer:
                grad_now, grad_cross = got[0], got[1]
                if step == 1:
                    first_grad_cross = grad_cross
                if step < outer - 1:
                    flying_b = (ring(grad_now, 1), cross(grad_now))
                else:
                    flying_b = (ring(first_grad_cross, outer - 1),)
            else:
                grad_now, grad_cross = None, got[0]
        grad_rows = [g for g in (grad_now, grad_cross) if g is not None]
        grad_block = grad_rows[0] if len(grad_rows) == 1 else jnp.concatenate(grad_rows, axis=0)
        result = backward(linear, grad_block)
        results.append((token_block, grad_block) + result)
        if step < outer:
            got = tie(*flying_a, *result)
            results[-1] = (token_block, grad_block) + tuple(got[-4:])
            if step < outer - 1:
                token_now, token_cross = got[0], got[1]
                if step + 1 < outer - 1:
                    flying_a = (ring(token_now, 1), cross(token_now))
                else:
                    flying_a = (cross(token_now),)
            else:
                token_now, token_cross = None, got[0]

    own = [results[s][2][:rows] for s in range(outer)]
    other = [results[s + 1][2][-rows:] for s in range(outer)]
    order = [s for s in range(outer - 1, 0, -1)] + [0]
    total = None
    for s in order:
        both = own[s].astype(F32) + cross(other[s]).astype(F32)
        if s:
            both = ring(both.astype(BF), outer - s).astype(F32)
        total = both if total is None else total + both
    grad_input = total.astype(BF)

    load = sum(
        jnp.sum(r[1][:, width:].astype(F32), axis=0, keepdims=True) for r in results
    )
    bit = 1
    while bit < groups:
        load = load + swap(load, bit)
        bit *= 2
    expert_load = load[0, :num_experts] * (num_experts / (rows * devices * groups * top_count))

    all_tokens = jnp.concatenate([r[0] for r in results], axis=0)
    all_delta = jnp.concatenate([r[3] for r in results], axis=0)
    all_hidden = jnp.concatenate([r[4] for r in results], axis=0)
    all_cotangent = jnp.concatenate([r[5] for r in results], axis=0)
    grad_gate_up = dot(all_tokens, all_delta, 0, 0).astype(BF)
    grad_down = dot(all_hidden, all_cotangent, 0, 0).astype(BF)

    def reduce_groups(value):
        bit = 1
        size = groups
        index = my_group
        while size > 1:
            value = value.reshape((size // 2, 2) + value.shape[1:])
            low = index % 2
            mine = lax.dynamic_index_in_dim(value, low, 1, keepdims=False)
            theirs = lax.dynamic_index_in_dim(value, 1 - low, 1, keepdims=False)
            summed = mine.astype(F32) + swap(theirs, bit).astype(F32)
            size //= 2
            index = index // 2
            bit *= 2
            value = summed.astype(BF) if size > 1 else summed
        return value[0] * (1.0 / groups)

    mine = reduce_groups(grad_gate_up.reshape(groups, width // groups, 2 * inner_width)).astype(BF)
    mine = mine.reshape(width // groups, 2, local_experts, hidden)
    out_gate = mine[:, 0].transpose(1, 0, 2)
    out_up = mine[:, 1].transpose(1, 0, 2)
    down_chunks = grad_down.reshape(local_experts, groups, hidden // groups, width).transpose(1, 0, 2, 3)
    out_down = reduce_groups(down_chunks).astype(BF)
    return (grad_input, out_gate, out_up, out_down, expert_load)


def solution(mesh):
    return jax.shard_map(
        shards,
        mesh=mesh,
        in_specs=(
            P(("expert", "dp"), None),
            P(("expert", "dp"), None),
            P(("expert", "dp"), None),
            P(("expert", "dp"), None),
            P("expert", None, None),
            P("expert", None, None),
            P("expert", None, None),
        ),
        out_specs=(
            P(("expert", "dp"), None),
            P("expert", "dp", None),
            P("expert", "dp", None),
            P("expert", "dp", None),
            P(),
        ),
        check_vma=False,
    )
```

```python
import jax
import jax.numpy as jnp
from jax import lax
from jax.sharding import PartitionSpec as P

BF = jnp.bfloat16
F32 = jnp.float32
LANES = 128


def dot(a, b, ca, cb):
    return lax.dot_general(a, b, (((ca,), (cb,)), ((), ())), preferred_element_type=F32)


def tie(*values):
    return lax.optimization_barrier(values)


def shards(tokens, out_grad, route_weights, expert_ids, gate_weight, up_weight, down_weight):
    local_experts, width, hidden = gate_weight.shape
    devices = lax.axis_size("expert")
    groups = lax.axis_size("dp")
    num_experts = local_experts * devices
    rows, top_count = expert_ids.shape
    outer = devices // 2
    inner_width = local_experts * hidden
    me = lax.axis_index("expert")
    my_group = lax.axis_index("dp")

    def ring(value, step):
        pairs = [(2 * z + x, 2 * ((z + step) % outer) + x) for z in range(outer) for x in range(2)]
        return lax.ppermute(value, "expert", pairs)

    def cross(value):
        return lax.ppermute(value, "expert", [(i, i ^ 1) for i in range(devices)])

    def swap(value, bit):
        return lax.ppermute(value, "dp", [(i, i ^ bit) for i in range(groups)])

    lanes = jnp.arange(LANES, dtype=jnp.int32)
    dense = jnp.sum(
        jnp.where(
            expert_ids[:, :, None] == lanes, route_weights.astype(F32)[:, :, None], 0.0
        ),
        axis=1,
    ).astype(BF)
    grads = jnp.concatenate([out_grad, dense], axis=1)

    gate_up = jnp.concatenate(
        [gate_weight[e] for e in range(local_experts)] + [up_weight[e] for e in range(local_experts)],
        axis=1,
    )
    down = down_weight.reshape(inner_width, width)

    def middle(linear, grad_rows):
        cotangent = grad_rows[:, :width]
        routes = grad_rows[:, width:].astype(F32)
        weight = jnp.concatenate(
            [
                jnp.broadcast_to(
                    jnp.sum(
                        jnp.where(lanes == me * local_experts + e, routes, 0.0), axis=1, keepdims=True
                    ),
                    (grad_rows.shape[0], hidden),
                )
                for e in range(local_experts)
            ],
            axis=1,
        )
        gate_linear = linear[:, :inner_width]
        up_linear = linear[:, inner_width:]
        delta_hidden = weight * dot(cotangent, down, 1, 1)
        logistic = jax.nn.sigmoid(gate_linear)
        activated = gate_linear * logistic
        scaled_hidden = (weight * activated * up_linear).astype(BF)
        delta_gate = delta_hidden * up_linear * logistic * (1.0 + gate_linear * (1.0 - logistic))
        delta_up = delta_hidden * activated
        delta = jnp.concatenate([delta_gate.astype(BF), delta_up.astype(BF)], axis=1)
        return delta, scaled_hidden

    def partial_input(delta):
        return dot(delta, gate_up, 1, 1).astype(BF)

    flying_a = (ring(tokens, 1), cross(tokens))
    flying_b = (ring(grads, 1), cross(grads))
    gate_up = tie(gate_up, grads)[0]
    token_blocks, grad_blocks, deltas, hiddens, partials = [], [], [], [], []
    first_grad_cross = None
    for step in range(1, outer):
        got = tie(*flying_a, *((deltas[-1], hiddens[-1], partials[-1]) if partials else ()))
        if partials:
            deltas[-1], hiddens[-1], partials[-1] = got[2:]
        flying_a = (cross(got[0]),) if step == outer - 1 else (ring(got[0], 1), cross(got[0]))
        here = ((tokens,) if step == 1 else ()) + tuple(got[:2])
        token_blocks.append(jnp.concatenate(here, axis=0))
        linear = dot(token_blocks[-1], gate_up, 1, 0)
        got = tie(*flying_b, linear)
        if step == 1:
            first_grad_cross = got[1]
        flying_b = (ring(first_grad_cross, outer - 1),) if step == outer - 1 else (ring(got[0], 1), cross(got[0]))
        here = ((grads,) if step == 1 else ()) + tuple(got[:2])
        grad_blocks.append(jnp.concatenate(here, axis=0))
        delta, scaled_hidden = middle(got[2], grad_blocks[-1])
        deltas.append(delta)
        hiddens.append(scaled_hidden)
        partials.append(partial_input(delta))

    def stacked(blocks):
        return jnp.concatenate(blocks, axis=0) if len(blocks) > 1 else blocks[0]

    def cotangents(blocks):
        return stacked([g[:, :width] for g in blocks])

    early_gate_up = dot(stacked(token_blocks[:-1]), stacked(deltas[:-1]), 0, 0).astype(BF)
    early_down = dot(stacked(hiddens[:-1]), cotangents(grad_blocks[:-1]), 0, 0).astype(BF)

    (last_tokens,) = flying_a
    last_tokens, early_gate_up, early_down = tie(last_tokens, early_gate_up, early_down)
    linear = dot(last_tokens, gate_up, 1, 0)
    got = tie(*flying_b, linear, deltas[-1], hiddens[-1], *partials)
    last_grads, linear, deltas[-1], hiddens[-1] = got[:4]
    partials = list(got[4:])
    own = [partials[0][:rows], partials[0][rows : 2 * rows]] + [p[:rows] for p in partials[1:]]
    other = [p[-rows:] for p in partials]

    order = list(range(outer - 2, 0, -1))
    crossed = {s: cross(other[s]) for s in order}
    token_blocks.append(last_tokens)
    grad_blocks.append(last_grads)
    load = sum(jnp.sum(g[:, width:].astype(F32), axis=0, keepdims=True) for g in grad_blocks)
    flying_load = swap(load, 1)
    delta, scaled_hidden = middle(linear, last_grads)
    deltas.append(delta)
    hiddens.append(scaled_hidden)

    late_tokens = stacked(token_blocks[-2:])
    late_grads = cotangents(grad_blocks[-2:])
    late_delta = stacked(deltas[-2:])
    late_hidden = stacked(hiddens[-2:])
    near, far = my_group, my_group ^ 2
    part = width // groups

    def gate_up_chunk(index, late_delta):
        columns = lax.dynamic_slice(late_tokens, (0, index * part), (late_tokens.shape[0], part))
        before = lax.dynamic_slice(early_gate_up, (index * part, 0), (part, early_gate_up.shape[1]))
        return (dot(columns, late_delta, 0, 0) + before.astype(F32)).astype(BF)

    def down_chunk(index):
        return lax.dynamic_index_in_dim(all_down, index, 1, keepdims=False)

    def add(a, b):
        return (a.astype(F32) + b.astype(F32)).astype(BF)

    all_down = (dot(late_hidden, late_grads, 0, 0) + early_down.astype(F32)).astype(BF)
    all_down, late_delta = tie(all_down, late_delta)
    all_down = all_down.reshape(local_experts, groups, hidden // groups, width)
    flying_down = swap(down_chunk(far ^ 1), 1)
    far_other = gate_up_chunk(far ^ 1, late_delta)
    flying_down, flying_load, far_other, late_delta, delta = tie(flying_down, flying_load, far_other, late_delta, delta)
    load = load + flying_load
    flying_load = swap(load, 2)
    flying_gate_up = swap(far_other, 1)
    far_down_sum = add(down_chunk(far), flying_down)
    flying_down = swap(far_down_sum, 2)
    far_mine = gate_up_chunk(far, late_delta)
    flying_gate_up, far_mine, delta, late_delta = tie(flying_gate_up, far_mine, delta, late_delta)
    far_sum = add(far_mine, flying_gate_up)
    flying_gate_up = swap(far_sum, 2)
    last_partial = partial_input(delta)
    near_other = gate_up_chunk(near ^ 1, late_delta)
    got = tie(far_sum, last_partial, near_other, late_delta, partials[0], *(crossed[s] for s in order))
    far_sum, last_partial, near_other, late_delta, first_partial = got[:5]
    crossed_last = cross(last_partial)
    near_gate_up = swap(near_other, 1)
    near_down = swap(down_chunk(near ^ 1), 1)
    back = []
    for s, value in zip(order, got[5:]):
        back.append(ring(add(own[s], value), outer - s))
    crossed_first = cross(first_partial[-rows:])
    near_mine = gate_up_chunk(near, late_delta)
    near_gate_up, near_down, near_mine, crossed_last = tie(near_gate_up, near_down, near_mine, crossed_last)
    back.append(ring(add(own[-1], crossed_last), 1))
    near_down = add(down_chunk(near), near_down)
    near_gate_up = add(near_mine, near_gate_up)
    got = tie(crossed_first, near_down, near_gate_up, *back)
    crossed_first, near_down, near_gate_up = got[:3]
    total = own[0].astype(F32) + crossed_first.astype(F32)
    for value in got[3:]:
        total = total + value.astype(F32)
    grad_input = total.astype(BF)
    flying_down, flying_load, grad_input, near_down = tie(flying_down, flying_load, grad_input, near_down)
    load = load + flying_load
    expert_load = load[0, :num_experts] * (num_experts / (rows * devices * groups * top_count))

    factor = 1.0 / groups
    out_down = ((near_down.astype(F32) + flying_down.astype(F32)) * factor).astype(BF)
    flying_gate_up, near_gate_up, out_down = tie(flying_gate_up, near_gate_up, out_down)
    out_gate, out_up = [], []
    for kind, out in ((0, out_gate), (1, out_up)):
        for e in range(local_experts):
            at = slice((kind * local_experts + e) * hidden, (kind * local_experts + e + 1) * hidden)
            value = near_gate_up[:, at].astype(F32) + flying_gate_up[:, at].astype(F32)
            out.append((value * factor).astype(BF))
    out_gate, out_up = jnp.stack(out_gate), jnp.stack(out_up)
    return (grad_input, out_gate, out_up, out_down, expert_load)


def solution(mesh):
    return jax.shard_map(
        shards,
        mesh=mesh,
        in_specs=(
            P(("expert", "dp"), None),
            P(("expert", "dp"), None),
            P(("expert", "dp"), None),
            P(("expert", "dp"), None),
            P("expert", None, None),
            P("expert", None, None),
            P("expert", None, None),
        ),
        out_specs=(
            P(("expert", "dp"), None),
            P("expert", "dp", None),
            P("expert", "dp", None),
            P("expert", "dp", None),
            P(),
        ),
        check_vma=False,
    )
```

```python
import jax
import jax.numpy as jnp
from jax import lax
from jax.sharding import PartitionSpec as P

BF = jnp.bfloat16
F32 = jnp.float32
LANES = 128


def dot(a, b, ca, cb):
    return lax.dot_general(a, b, (((ca,), (cb,)), ((), ())), preferred_element_type=F32)


def tie(*values):
    return lax.optimization_barrier(values)


def shards(tokens, out_grad, route_weights, expert_ids, gate_weight, up_weight, down_weight):
    local_experts, width, hidden = gate_weight.shape
    devices = lax.axis_size("expert")
    groups = lax.axis_size("dp")
    num_experts = local_experts * devices
    rows, top_count = expert_ids.shape
    outer = devices // 2
    inner_width = local_experts * hidden
    me = lax.axis_index("expert")
    my_group = lax.axis_index("dp")

    def ring(value, step):
        pairs = [(2 * z + x, 2 * ((z + step) % outer) + x) for z in range(outer) for x in range(2)]
        return lax.ppermute(value, "expert", pairs)

    def cross(value):
        return lax.ppermute(value, "expert", [(i, i ^ 1) for i in range(devices)])

    def swap(value, bit):
        return lax.ppermute(value, "dp", [(i, i ^ bit) for i in range(groups)])

    lanes = jnp.arange(LANES, dtype=jnp.int32)
    dense = jnp.sum(
        jnp.where(
            expert_ids[:, :, None] == lanes, route_weights.astype(F32)[:, :, None], 0.0
        ),
        axis=1,
    ).astype(BF)
    grads = jnp.concatenate([out_grad, dense], axis=1)

    gate_up = jnp.concatenate(
        [gate_weight[e] for e in range(local_experts)] + [up_weight[e] for e in range(local_experts)],
        axis=1,
    )
    down_matrix = down_weight.reshape(inner_width, width)

    def middle(linear, grad_rows):
        cotangent = grad_rows[:, :width]
        routes = grad_rows[:, width:].astype(F32)
        weight = jnp.concatenate(
            [
                jnp.broadcast_to(
                    jnp.sum(
                        jnp.where(lanes == me * local_experts + e, routes, 0.0), axis=1, keepdims=True
                    ),
                    (grad_rows.shape[0], hidden),
                )
                for e in range(local_experts)
            ],
            axis=1,
        )
        gate_linear = linear[:, :inner_width]
        up_linear = linear[:, inner_width:]
        delta_hidden = weight * dot(cotangent, down_matrix, 1, 1)
        logistic = jax.nn.sigmoid(gate_linear)
        activated = gate_linear * logistic
        scaled_hidden = (weight * activated * up_linear).astype(BF)
        delta_gate = delta_hidden * up_linear * logistic * (1.0 + gate_linear * (1.0 - logistic))
        delta_up = delta_hidden * activated
        delta = jnp.concatenate([delta_gate.astype(BF), delta_up.astype(BF)], axis=1)
        return delta, scaled_hidden

    def partial_input(delta):
        return dot(delta, gate_up, 1, 1).astype(BF)

    near = my_group
    chunk_order = [near ^ 3, near ^ 2, near ^ 1, near]
    part = width // groups

    def stacked(blocks, axis=0):
        return jnp.concatenate(blocks, axis=axis) if len(blocks) > 1 else blocks[0]

    def by_chunk(blocks):
        return [
            stacked([lax.dynamic_slice(b, (0, c * part), (b.shape[0], part)) for b in blocks]) for c in chunk_order
        ]

    def cotangents(blocks):
        return stacked([g[:, :width] for g in blocks])

    def add(a, b):
        return (a.astype(F32) + b.astype(F32)).astype(BF)

    flying_a = (ring(tokens, 1), cross(tokens))
    flying_b = (ring(grads, 1), cross(grads))
    gate_up = tie(gate_up, grads)[0]
    token_blocks, grad_blocks, deltas, hiddens, own, other = [], [], [], [], [], []
    first_grad_cross = None
    for step in range(1, outer):
        got = tie(*flying_a, *((deltas[-1], hiddens[-1], own[-1], other[-1], first_grad_cross) if own else ()))
        if own:
            deltas[-1], hiddens[-1], own[-1], other[-1], first_grad_cross = got[2:]
        if step == outer - 1:
            flying_a = (cross(got[0]),)
            flying_back = (ring(first_grad_cross, outer - 1),)
        else:
            flying_a = (ring(got[0], 1), cross(got[0]))
        new_tokens = ((tokens,) if step == 1 else ()) + tuple(got[:2])
        token_blocks.append(new_tokens)
        linear = dot(stacked(new_tokens), gate_up, 1, 0)
        got = tie(*flying_b, linear)
        if step == 1:
            first_grad_cross = got[1]
        flying_b = flying_back if step == outer - 1 else (ring(got[0], 1), cross(got[0]))
        new_grads = ((grads,) if step == 1 else ()) + tuple(got[:2])
        grad_blocks.append(new_grads)
        delta, scaled_hidden = middle(got[2], stacked(new_grads))
        deltas.append(delta)
        hiddens.append(scaled_hidden)
        partial = partial_input(delta)
        if step == 1:
            own.append(partial[:rows])
        own.append(partial[-2 * rows : -rows])
        other.append(partial[-rows:])

    early = [t for blocks in token_blocks[:-1] for t in blocks]
    early_delta = stacked(deltas[:-1])
    early_gate_up = [dot(c, early_delta, 0, 0).astype(BF) for c in by_chunk(early)]
    early_down = dot(stacked(hiddens[:-1]), cotangents([g for b in grad_blocks[:-1] for g in b]), 0, 0).astype(BF)
    late_columns = by_chunk(token_blocks[-1])

    got = tie(*flying_a, early_down, *early_gate_up, *late_columns, *own, *other)
    last_tokens, early_down = got[:2]
    early_gate_up, late_columns = got[2 : 2 + groups], got[2 + groups : 2 + 2 * groups]
    own, other = got[2 + 2 * groups : 2 + 2 * groups + outer], got[2 + 2 * groups + outer :]
    crossed = {s: cross(other[s]) for s in range(1, outer - 1)}
    late_columns = [stacked([a, b]) for a, b in zip(late_columns, by_chunk([last_tokens]))]
    linear = dot(last_tokens, gate_up, 1, 0)
    got = tie(*flying_b, linear, deltas[-1], hiddens[-1], *late_columns)
    last_grads, linear, deltas[-1], hiddens[-1] = got[:4]
    late_columns = got[4:]
    grad_blocks.append((last_grads,))
    load = sum(jnp.sum(g[:, width:].astype(F32), axis=0, keepdims=True) for b in grad_blocks for g in b)
    flying_load = swap(load, 1)
    delta, scaled_hidden = middle(linear, last_grads)
    late_delta = stacked([deltas[-1], delta])
    late_hidden = stacked([hiddens[-1], scaled_hidden])
    late_grads = cotangents([g for b in grad_blocks[-2:] for g in b])

    def gate_up_chunk(index, late_delta, received=None):
        value = dot(late_columns[index], late_delta, 0, 0) + early_gate_up[index].astype(F32)
        return (value if received is None else value + received.astype(F32)).astype(BF)

    def joined(gate_up_part, down_part):
        parts = [gate_up_part[:, i : i + part] for i in range(0, gate_up_part.shape[1], part)]
        down_part = down_part.reshape(-1, width)
        parts += [down_part[:, i : i + part] for i in range(0, width, part)]
        return jnp.concatenate(parts, axis=0)

    def split(message):
        count = 2 * inner_width // part
        wide = jnp.concatenate([message[i * part : (i + 1) * part] for i in range(count)], axis=1)
        rest = message[count * part :]
        size = rest.shape[0] // groups
        narrow = jnp.concatenate([rest[i * size : (i + 1) * size] for i in range(groups)], axis=1)
        return wide, narrow.reshape(local_experts, hidden // groups, width)

    far_other = gate_up_chunk(0, late_delta)
    flying_gate_up = swap(far_other, 1)
    far_other, late_hidden, late_delta = tie(far_other, late_hidden, late_delta)
    all_down = dot(late_hidden, late_grads, 0, 0) + early_down.astype(F32)
    all_down = all_down.astype(BF).reshape(local_experts, groups, hidden // groups, width)
    down = [lax.dynamic_index_in_dim(all_down, c, 1, keepdims=False) for c in chunk_order]
    flying_down = swap(down[0], 1)
    flying_gate_up, flying_load, late_delta, delta, *down = tie(flying_gate_up, flying_load, late_delta, delta, *down)
    far_sum = gate_up_chunk(1, late_delta, flying_gate_up)
    far_sum, flying_down, load, delta, late_delta = tie(far_sum, flying_down, load + flying_load, delta, late_delta)
    flying_load = swap(load, 2)
    message = joined(far_sum, add(down[1], flying_down))
    flying_far = swap(message, 2)
    got = tie(message, delta, late_delta, down[2], other[0], flying_load, crossed[1])
    _, delta, late_delta, near_down, first_other, flying_load, hop = got
    hop = ring(add(own[1], hop), 1)
    last_partial = partial_input(delta)
    crossed[outer - 1] = cross(last_partial)
    near_other = gate_up_chunk(2, late_delta)
    near_gate_up = swap(near_other, 1)
    near_down = swap(near_down, 1)
    near_gate_up, near_down, late_delta = tie(near_gate_up, near_down, late_delta)
    near_gate_up = gate_up_chunk(3, late_delta, near_gate_up)
    near_down = add(down[3], near_down)
    for s in range(2, outer):
        if s == outer - 1:
            hop, crossed[s], near_gate_up, near_down = tie(hop, crossed[s], near_gate_up, near_down)
            crossed[0] = cross(first_other)
        else:
            hop, crossed[s] = tie(hop, crossed[s])
        hop = (own[s].astype(F32) + crossed[s].astype(F32) + hop.astype(F32)).astype(BF)
        hop = ring(hop, 1)
    hop, crossed[0] = tie(hop, crossed[0])
    grad_input = (own[0].astype(F32) + crossed[0].astype(F32) + hop.astype(F32)).astype(BF)

    load = load + flying_load
    expert_load = load[0, :num_experts] * (num_experts / (rows * devices * groups * top_count))
    factor = 1.0 / groups
    flying_far, near_gate_up, near_down, grad_input = tie(flying_far, near_gate_up, near_down, grad_input)
    far_gate_up, far_down = split(flying_far)
    out_gate, out_up = [], []
    for kind, out in ((0, out_gate), (1, out_up)):
        for e in range(local_experts):
            at = slice((kind * local_experts + e) * hidden, (kind * local_experts + e + 1) * hidden)
            value = near_gate_up[:, at].astype(F32) + far_gate_up[:, at].astype(F32)
            out.append((value * factor).astype(BF))
    out_gate, out_up = jnp.stack(out_gate), jnp.stack(out_up)
    out_down = ((near_down.astype(F32) + far_down.astype(F32)) * factor).astype(BF)
    return (grad_input, out_gate, out_up, out_down, expert_load)


def solution(mesh):
    return jax.shard_map(
        shards,
        mesh=mesh,
        in_specs=(
            P(("expert", "dp"), None),
            P(("expert", "dp"), None),
            P(("expert", "dp"), None),
            P(("expert", "dp"), None),
            P("expert", None, None),
            P("expert", None, None),
            P("expert", None, None),
        ),
        out_specs=(
            P(("expert", "dp"), None),
            P("expert", "dp", None),
            P("expert", "dp", None),
            P("expert", "dp", None),
            P(),
        ),
        check_vma=False,
    )
```

```python
import jax
import jax.numpy as jnp
from jax import lax
from jax.sharding import PartitionSpec as P

BF = jnp.bfloat16
F32 = jnp.float32
LANES = 128


def dot(a, b, ca, cb):
    return lax.dot_general(a, b, (((ca,), (cb,)), ((), ())), preferred_element_type=F32)


def tie(*values):
    return lax.optimization_barrier(values)


def shards(tokens, out_grad, route_weights, expert_ids, gate_weight, up_weight, down_weight):
    local_experts, width, hidden = gate_weight.shape
    devices = lax.axis_size("expert")
    groups = lax.axis_size("dp")
    num_experts = local_experts * devices
    rows, top_count = expert_ids.shape
    outer = devices // 2
    inner_width = local_experts * hidden
    me = lax.axis_index("expert")
    my_group = lax.axis_index("dp")

    def ring(value, step):
        pairs = [(2 * z + x, 2 * ((z + step) % outer) + x) for z in range(outer) for x in range(2)]
        return lax.ppermute(value, "expert", pairs)

    def cross(value):
        return lax.ppermute(value, "expert", [(i, i ^ 1) for i in range(devices)])

    def swap(value, bit):
        return lax.ppermute(value, "dp", [(i, i ^ bit) for i in range(groups)])

    lanes = jnp.arange(LANES, dtype=jnp.int32)
    dense = jnp.sum(
        jnp.where(
            expert_ids[:, :, None] == lanes, route_weights.astype(F32)[:, :, None], 0.0
        ),
        axis=1,
    ).astype(BF)
    grads = jnp.concatenate([out_grad, dense], axis=1)

    gate_up = jnp.concatenate(
        [gate_weight[e] for e in range(local_experts)] + [up_weight[e] for e in range(local_experts)],
        axis=1,
    )
    down_matrix = down_weight.reshape(inner_width, width)

    def middle(linear, grad_rows):
        cotangent = grad_rows[:, :width]
        routes = grad_rows[:, width:].astype(F32)
        weight = jnp.concatenate(
            [
                jnp.broadcast_to(
                    jnp.sum(
                        jnp.where(lanes == me * local_experts + e, routes, 0.0), axis=1, keepdims=True
                    ),
                    (grad_rows.shape[0], hidden),
                )
                for e in range(local_experts)
            ],
            axis=1,
        )
        gate_linear = linear[:, :inner_width]
        up_linear = linear[:, inner_width:]
        delta_hidden = weight * dot(cotangent, down_matrix, 1, 1)
        logistic = jax.nn.sigmoid(gate_linear)
        activated = gate_linear * logistic
        scaled_hidden = (weight * activated * up_linear).astype(BF)
        delta_gate = delta_hidden * up_linear * logistic * (1.0 + gate_linear * (1.0 - logistic))
        delta_up = delta_hidden * activated
        delta = jnp.concatenate([delta_gate.astype(BF), delta_up.astype(BF)], axis=1)
        return delta, scaled_hidden

    def partial_input(delta):
        return dot(delta, gate_up, 1, 1).astype(BF)

    near = my_group
    chunk_order = [near ^ 3, near ^ 2, near ^ 1, near]
    part = width // groups

    def stacked(blocks, axis=0):
        return jnp.concatenate(blocks, axis=axis) if len(blocks) > 1 else blocks[0]

    def by_chunk(blocks):
        return [
            stacked([lax.dynamic_slice(b, (0, c * part), (b.shape[0], part)) for b in blocks]) for c in chunk_order
        ]

    def cotangents(blocks):
        return stacked([g[:, :width] for g in blocks])

    def add(a, b):
        return (a.astype(F32) + b.astype(F32)).astype(BF)

    flying_a = (ring(tokens, 1), cross(tokens))
    flying_b = (ring(grads, 1), cross(grads))
    gate_up = tie(gate_up, grads)[0]
    token_blocks, grad_blocks, deltas, hiddens, own, other = [], [], [], [], [], []
    first_grad_cross = None
    for step in range(1, outer):
        got = tie(*flying_a, *((deltas[-1], hiddens[-1], own[-1], other[-1], first_grad_cross) if own else ()))
        if own:
            deltas[-1], hiddens[-1], own[-1], other[-1], first_grad_cross = got[2:]
        if step == outer - 1:
            flying_a = (cross(got[0]),)
            flying_back = (ring(first_grad_cross, outer - 1),)
        else:
            flying_a = (ring(got[0], 1), cross(got[0]))
        new_tokens = ((tokens,) if step == 1 else ()) + tuple(got[:2])
        token_blocks.append(new_tokens)
        linear = dot(stacked(new_tokens), gate_up, 1, 0)
        got = tie(*flying_b, linear)
        if step == 1:
            first_grad_cross = got[1]
        flying_b = flying_back if step == outer - 1 else (ring(got[0], 1), cross(got[0]))
        new_grads = ((grads,) if step == 1 else ()) + tuple(got[:2])
        grad_blocks.append(new_grads)
        delta, scaled_hidden = middle(got[2], stacked(new_grads))
        deltas.append(delta)
        hiddens.append(scaled_hidden)
        partial = partial_input(delta)
        if step == 1:
            own.append(partial[:rows])
        own.append(partial[-2 * rows : -rows])
        other.append(partial[-rows:])

    early = [t for blocks in token_blocks[:-1] for t in blocks]
    early_delta = stacked(deltas[:-1])
    early_gate_up = [dot(c, early_delta, 0, 0).astype(BF) for c in by_chunk(early)]
    early_down = dot(stacked(hiddens[:-1]), cotangents([g for b in grad_blocks[:-1] for g in b]), 0, 0).astype(BF)
    late_columns = by_chunk(token_blocks[-1])

    last_tokens, *got = tie(*flying_a, *own, *other)
    own, other = got[:outer], got[outer:]
    middle_step = outer // 2
    order = list(range(middle_step, 0, -1)) + list(range(middle_step + 1, outer - 1))
    crossed = {s: cross(other[s]) for s in order}
    late_columns = [stacked([a, b]) for a, b in zip(late_columns, by_chunk([last_tokens]))]
    linear = dot(last_tokens, gate_up, 1, 0)
    got = tie(*flying_b, linear, deltas[-1], hiddens[-1], early_down, *early_gate_up, *late_columns)
    last_grads, linear, deltas[-1], hiddens[-1], early_down = got[:5]
    early_gate_up, late_columns = got[5 : 5 + groups], got[5 + groups :]
    grad_blocks.append((last_grads,))
    load = sum(jnp.sum(g[:, width:].astype(F32), axis=0, keepdims=True) for b in grad_blocks for g in b)
    flying_load = swap(load, 1)
    delta, scaled_hidden = middle(linear, last_grads)
    late_delta = stacked([deltas[-1], delta])
    late_hidden = stacked([hiddens[-1], scaled_hidden])
    late_grads = cotangents([g for b in grad_blocks[-2:] for g in b])

    def chunk(index, late_delta, kind, received=None):
        columns = slice(kind * inner_width, (kind + 1) * inner_width)
        value = dot(late_columns[index], late_delta[:, columns], 0, 0) + early_gate_up[index][:, columns].astype(F32)
        return (value if received is None else value + received.astype(F32)).astype(BF)

    def joined(up_part, down_part):
        size = part // 2
        down_part = down_part.reshape(-1, width)
        parts = [v[:, i : i + size] for v in (up_part, down_part) for i in range(0, v.shape[1], size)]
        return jnp.concatenate(parts, axis=0)

    def split(message):
        size = part // 2
        count = inner_width // size
        wide = jnp.concatenate([message[i * part : (i + 1) * part] for i in range(count)], axis=1)
        rest = message[count * part :]
        tall = local_experts * hidden // groups
        narrow = jnp.concatenate([rest[i * tall : (i + 1) * tall] for i in range(width // size)], axis=1)
        return wide, narrow.reshape(local_experts, hidden // groups, width)

    far_gate = chunk(0, late_delta, 0)
    flying_gate = swap(far_gate, 1)
    far_gate, late_delta = tie(far_gate, late_delta)
    far_up = chunk(0, late_delta, 1)
    flying_up = swap(far_up, 1)
    far_up, late_delta, flying_gate, flying_load = tie(far_up, late_delta, flying_gate, flying_load)
    load = load + flying_load
    flying_load = swap(load, 2)
    gate_sum = chunk(1, late_delta, 0, flying_gate)
    flying_gate = swap(gate_sum, 2)
    gate_sum, late_hidden, late_grads, late_delta, value = tie(
        gate_sum, late_hidden, late_grads, late_delta, crossed[middle_step]
    )
    minus = ring(add(own[middle_step], value), outer - 1)
    all_down = (dot(late_hidden, late_grads, 0, 0) + early_down.astype(F32)).astype(BF)
    all_down = all_down.reshape(local_experts, groups, hidden // groups, width)
    down = [lax.dynamic_index_in_dim(all_down, c, 1, keepdims=False) for c in chunk_order]
    flying_down = swap(down[0], 1)
    flying_up, late_delta, delta, *down = tie(flying_up, late_delta, delta, *down)
    up_sum = chunk(1, late_delta, 1, flying_up)
    up_sum, flying_down, delta, late_delta = tie(up_sum, flying_down, delta, late_delta)
    message = joined(up_sum, add(down[1], flying_down))
    flying_far = swap(message, 2)
    message, delta, late_delta, near_down, first_other = tie(message, delta, late_delta, down[2], other[0])
    last_partial = partial_input(delta)
    crossed[outer - 1] = cross(last_partial)
    near_gate = swap(chunk(2, late_delta, 0), 1)
    near_up = swap(chunk(2, late_delta, 1), 1)
    near_down = swap(near_down, 1)
    crossed[0] = cross(first_other)
    near_gate, near_up, near_down, late_delta = tie(near_gate, near_up, near_down, late_delta)
    near_gate = chunk(3, late_delta, 0, near_gate)
    near_up = chunk(3, late_delta, 1, near_up)
    near_down = add(down[3], near_down)
    plus = None
    for s in range(middle_step - 1, 0, -1):
        minus, crossed[s], near_gate, near_up, near_down = tie(minus, crossed[s], near_gate, near_up, near_down)
        minus = ring((own[s].astype(F32) + crossed[s].astype(F32) + minus.astype(F32)).astype(BF), outer - 1)
    for s in range(middle_step + 1, outer):
        if plus is None:
            crossed[s], near_gate = tie(crossed[s], near_gate)
            plus = own[s].astype(F32) + crossed[s].astype(F32)
        else:
            crossed[s], plus, near_gate = tie(crossed[s], plus, near_gate)
            plus = own[s].astype(F32) + crossed[s].astype(F32) + plus.astype(F32)
        plus = ring(plus.astype(BF), 1)

    factor = 1.0 / groups

    def outputs(near, far):
        halves = []
        for e in range(local_experts):
            at = slice(e * hidden, (e + 1) * hidden)
            halves.append(((near[:, at].astype(F32) + far[:, at].astype(F32)) * factor).astype(BF))
        return jnp.stack(halves)

    flying_gate, near_gate = tie(flying_gate, near_gate)
    out_gate = outputs(near_gate, flying_gate)
    minus, plus, crossed[0], out_gate = tie(minus, plus, crossed[0], out_gate)
    grad_input = (
        own[0].astype(F32) + crossed[0].astype(F32) + minus.astype(F32) + plus.astype(F32)
    ).astype(BF)
    flying_far, flying_load, near_up, near_down, grad_input = tie(
        flying_far, flying_load, near_up, near_down, grad_input
    )
    load = load + flying_load
    expert_load = load[0, :num_experts] * (num_experts / (rows * devices * groups * top_count))
    far_up, far_down = split(flying_far)
    out_up = outputs(near_up, far_up)
    out_down = ((near_down.astype(F32) + far_down.astype(F32)) * factor).astype(BF)
    return (grad_input, out_gate, out_up, out_down, expert_load)


def solution(mesh):
    return jax.shard_map(
        shards,
        mesh=mesh,
        in_specs=(
            P(("expert", "dp"), None),
            P(("expert", "dp"), None),
            P(("expert", "dp"), None),
            P(("expert", "dp"), None),
            P("expert", None, None),
            P("expert", None, None),
            P("expert", None, None),
        ),
        out_specs=(
            P(("expert", "dp"), None),
            P("expert", "dp", None),
            P("expert", "dp", None),
            P("expert", "dp", None),
            P(),
        ),
        check_vma=False,
    )
```

```python
import jax
import jax.numpy as jnp
from jax import lax
from jax.sharding import PartitionSpec as P

BF = jnp.bfloat16
F32 = jnp.float32
LANES = 128


def dot(a, b, ca, cb):
    return lax.dot_general(a, b, (((ca,), (cb,)), ((), ())), preferred_element_type=F32)


def tie(*values):
    return lax.optimization_barrier(values)


def shards(tokens, out_grad, route_weights, expert_ids, gate_weight, up_weight, down_weight):
    local_experts, width, hidden = gate_weight.shape
    devices = lax.axis_size("expert")
    groups = lax.axis_size("dp")
    num_experts = local_experts * devices
    rows, top_count = expert_ids.shape
    outer = devices // 2
    inner_width = local_experts * hidden
    me = lax.axis_index("expert")
    my_group = lax.axis_index("dp")

    def ring(value, step):
        pairs = [(2 * z + x, 2 * ((z + step) % outer) + x) for z in range(outer) for x in range(2)]
        return lax.ppermute(value, "expert", pairs)

    def cross(value):
        return lax.ppermute(value, "expert", [(i, i ^ 1) for i in range(devices)])

    def swap(value, bit):
        return lax.ppermute(value, "dp", [(i, i ^ bit) for i in range(groups)])

    lanes = jnp.arange(LANES, dtype=jnp.int32)
    dense = jnp.sum(
        jnp.where(
            expert_ids[:, :, None] == lanes, route_weights.astype(F32)[:, :, None], 0.0
        ),
        axis=1,
    ).astype(BF)
    grads = jnp.concatenate([out_grad, dense], axis=1)

    gate_up = jnp.concatenate(
        [gate_weight[e] for e in range(local_experts)] + [up_weight[e] for e in range(local_experts)],
        axis=1,
    )
    down_matrix = down_weight.reshape(inner_width, width)

    def middle(linear, grad_rows):
        cotangent = grad_rows[:, :width]
        routes = grad_rows[:, width:].astype(F32)
        weight = jnp.concatenate(
            [
                jnp.broadcast_to(
                    jnp.sum(
                        jnp.where(lanes == me * local_experts + e, routes, 0.0), axis=1, keepdims=True
                    ),
                    (grad_rows.shape[0], hidden),
                )
                for e in range(local_experts)
            ],
            axis=1,
        )
        gate_linear = linear[:, :inner_width]
        up_linear = linear[:, inner_width:]
        delta_hidden = weight * dot(cotangent, down_matrix, 1, 1)
        logistic = jax.nn.sigmoid(gate_linear)
        activated = gate_linear * logistic
        scaled_hidden = (weight * activated * up_linear).astype(BF)
        delta_gate = delta_hidden * up_linear * logistic * (1.0 + gate_linear * (1.0 - logistic))
        delta_up = delta_hidden * activated
        delta = jnp.concatenate([delta_gate.astype(BF), delta_up.astype(BF)], axis=1)
        return delta, scaled_hidden

    def partial_input(delta):
        return dot(delta, gate_up, 1, 1).astype(BF)

    near = my_group
    chunk_order = [near ^ 3, near ^ 2, near ^ 1, near]
    part = width // groups

    def stacked(blocks, axis=0):
        return jnp.concatenate(blocks, axis=axis) if len(blocks) > 1 else blocks[0]

    def by_chunk(blocks):
        return [
            stacked([lax.dynamic_slice(b, (0, c * part), (b.shape[0], part)) for b in blocks]) for c in chunk_order
        ]

    def cotangents(blocks):
        return stacked([g[:, :width] for g in blocks])

    def add(a, b):
        return (a.astype(F32) + b.astype(F32)).astype(BF)

    flying_a = (ring(tokens, 1), cross(tokens))
    flying_b = (ring(grads, 1), cross(grads))
    gate_up = tie(gate_up, grads)[0]
    token_blocks, grad_blocks, deltas, hiddens, own, other = [], [], [], [], [], []
    first_grad_cross = None
    for step in range(1, outer):
        got = tie(*flying_a, *((deltas[-1], hiddens[-1], own[-1], other[-1], first_grad_cross) if own else ()))
        if own:
            deltas[-1], hiddens[-1], own[-1], other[-1], first_grad_cross = got[2:]
        if step == outer - 1:
            flying_a = (cross(got[0]),)
            flying_back = (ring(first_grad_cross, outer - 1),)
        else:
            flying_a = (ring(got[0], 1), cross(got[0]))
        new_tokens = ((tokens,) if step == 1 else ()) + tuple(got[:2])
        token_blocks.append(new_tokens)
        linear = dot(stacked(new_tokens), gate_up, 1, 0)
        got = tie(*flying_b, linear)
        if step == 1:
            first_grad_cross = got[1]
        flying_b = flying_back if step == outer - 1 else (ring(got[0], 1), cross(got[0]))
        new_grads = ((grads,) if step == 1 else ()) + tuple(got[:2])
        grad_blocks.append(new_grads)
        delta, scaled_hidden = middle(got[2], stacked(new_grads))
        deltas.append(delta)
        hiddens.append(scaled_hidden)
        partial = partial_input(delta)
        if step == 1:
            own.append(partial[:rows])
        own.append(partial[-2 * rows : -rows])
        other.append(partial[-rows:])

    early = [t for blocks in token_blocks[:-1] for t in blocks]
    early_delta = stacked(deltas[:-1])
    early_gate_up = [dot(c, early_delta, 0, 0).astype(BF) for c in by_chunk(early)]
    early_down = dot(stacked(hiddens[:-1]), cotangents([g for b in grad_blocks[:-1] for g in b]), 0, 0).astype(BF)
    late_columns = by_chunk(token_blocks[-1])

    last_tokens, *got = tie(*flying_a, *own, *other)
    own, other = got[:outer], got[outer:]
    middle_step = outer // 2
    order = list(range(middle_step, 0, -1)) + list(range(middle_step + 1, outer - 1))
    crossed = {s: cross(other[s]) for s in order}
    late_columns = [stacked([a, b]) for a, b in zip(late_columns, by_chunk([last_tokens]))]
    linear = dot(last_tokens, gate_up, 1, 0)
    got = tie(*flying_b, linear, deltas[-1], hiddens[-1], early_down, *early_gate_up, *late_columns)
    last_grads, linear, deltas[-1], hiddens[-1], early_down = got[:5]
    early_gate_up, late_columns = got[5 : 5 + groups], got[5 + groups :]
    grad_blocks.append((last_grads,))
    load = sum(jnp.sum(g[:, width:].astype(F32), axis=0, keepdims=True) for b in grad_blocks for g in b)
    flying_load = swap(load, 1)
    delta, scaled_hidden = middle(linear, last_grads)
    late_delta = stacked([deltas[-1], delta])
    late_hidden = stacked([hiddens[-1], scaled_hidden])
    late_grads = cotangents([g for b in grad_blocks[-2:] for g in b])

    def chunk(index, late_delta, kind, received=None):
        columns = slice(kind * inner_width, (kind + 1) * inner_width)
        value = dot(late_columns[index], late_delta[:, columns], 0, 0) + early_gate_up[index][:, columns].astype(F32)
        return (value if received is None else value + received.astype(F32)).astype(BF)

    def joined(*values):
        size = part // 2
        values = [v.reshape(-1, v.shape[-1]) for v in values]
        return jnp.concatenate([v[:, i : i + size] for v in values for i in range(0, v.shape[1], size)], axis=0)

    def split(message):
        size = part // 2
        out = []
        for tall, wide in ((part, inner_width), (part, inner_width), (local_experts * hidden // groups, width)):
            count = wide // size
            out.append(jnp.concatenate([message[i * tall : (i + 1) * tall] for i in range(count)], axis=1))
            message = message[count * tall :]
        return out[0], out[1], out[2].reshape(local_experts, hidden // groups, width)

    far_gate = chunk(0, late_delta, 0)
    flying_gate = swap(far_gate, 1)
    far_gate, late_delta = tie(far_gate, late_delta)
    far_up = chunk(0, late_delta, 1)
    flying_up = swap(far_up, 1)
    all_down = (dot(late_hidden, late_grads, 0, 0) + early_down.astype(F32)).astype(BF)
    all_down = all_down.reshape(local_experts, groups, hidden // groups, width)
    down = [lax.dynamic_index_in_dim(all_down, c, 1, keepdims=False) for c in chunk_order]
    flying_down = swap(down[0], 1)
    flying_gate, flying_load, far_up, late_delta, *down = tie(flying_gate, flying_load, far_up, late_delta, *down)
    load = load + flying_load
    flying_load = swap(load, 2)
    gate_sum = chunk(1, late_delta, 0, flying_gate)
    flying_up, gate_sum, late_delta = tie(flying_up, gate_sum, late_delta)
    up_sum = chunk(1, late_delta, 1, flying_up)
    flying_down, gate_sum, up_sum, late_delta, delta = tie(flying_down, gate_sum, up_sum, late_delta, delta)
    message = joined(gate_sum, up_sum, add(down[1], flying_down))
    flying_far = swap(message, 2)
    message, delta, late_delta, near_down, first_other = tie(message, delta, late_delta, down[2], other[0])
    last_partial = partial_input(delta)
    crossed[outer - 1] = cross(last_partial)
    last_partial, late_delta, value = tie(last_partial, late_delta, crossed[middle_step])
    minus = ring(add(own[middle_step], value), outer - 1)
    near_gate = swap(chunk(2, late_delta, 0), 1)
    near_up = swap(chunk(2, late_delta, 1), 1)
    near_down = swap(near_down, 1)
    crossed[0] = cross(first_other)
    near_gate, near_up, near_down, late_delta = tie(near_gate, near_up, near_down, late_delta)
    near_gate = chunk(3, late_delta, 0, near_gate)
    near_up = chunk(3, late_delta, 1, near_up)
    near_down = add(down[3], near_down)
    plus = None
    for s in range(middle_step - 1, 0, -1):
        minus, crossed[s], near_gate, near_up, near_down = tie(minus, crossed[s], near_gate, near_up, near_down)
        minus = ring((own[s].astype(F32) + crossed[s].astype(F32) + minus.astype(F32)).astype(BF), outer - 1)
    for s in range(middle_step + 1, outer):
        if plus is None:
            crossed[s], near_gate = tie(crossed[s], near_gate)
            plus = own[s].astype(F32) + crossed[s].astype(F32)
        else:
            crossed[s], plus, near_gate = tie(crossed[s], plus, near_gate)
            plus = own[s].astype(F32) + crossed[s].astype(F32) + plus.astype(F32)
        plus = ring(plus.astype(BF), 1)

    factor = 1.0 / groups

    def outputs(near, far):
        halves = []
        for e in range(local_experts):
            at = slice(e * hidden, (e + 1) * hidden)
            halves.append(((near[:, at].astype(F32) + far[:, at].astype(F32)) * factor).astype(BF))
        return jnp.stack(halves)

    minus, plus, crossed[0] = tie(minus, plus, crossed[0])
    grad_input = (
        own[0].astype(F32) + crossed[0].astype(F32) + minus.astype(F32) + plus.astype(F32)
    ).astype(BF)
    flying_far, flying_load, near_gate, near_up, near_down, grad_input = tie(
        flying_far, flying_load, near_gate, near_up, near_down, grad_input
    )
    load = load + flying_load
    expert_load = load[0, :num_experts] * (num_experts / (rows * devices * groups * top_count))
    far_gate, far_up, far_down = split(flying_far)
    out_gate = outputs(near_gate, far_gate)
    out_up = outputs(near_up, far_up)
    out_down = ((near_down.astype(F32) + far_down.astype(F32)) * factor).astype(BF)
    return (grad_input, out_gate, out_up, out_down, expert_load)


def solution(mesh):
    return jax.shard_map(
        shards,
        mesh=mesh,
        in_specs=(
            P(("expert", "dp"), None),
            P(("expert", "dp"), None),
            P(("expert", "dp"), None),
            P(("expert", "dp"), None),
            P("expert", None, None),
            P("expert", None, None),
            P("expert", None, None),
        ),
        out_specs=(
            P(("expert", "dp"), None),
            P("expert", "dp", None),
            P("expert", "dp", None),
            P("expert", "dp", None),
            P(),
        ),
        check_vma=False,
    )
```

```python
import jax
import jax.numpy as jnp
from jax import lax
from jax.sharding import PartitionSpec as P

BF = jnp.bfloat16
F32 = jnp.float32
LANES = 128


def dot(a, b, ca, cb):
    return lax.dot_general(a, b, (((ca,), (cb,)), ((), ())), preferred_element_type=F32)


def tie(*values):
    return lax.optimization_barrier(values)


def shards(tokens, out_grad, route_weights, expert_ids, gate_weight, up_weight, down_weight):
    local_experts, width, hidden = gate_weight.shape
    devices = lax.axis_size("expert")
    groups = lax.axis_size("dp")
    num_experts = local_experts * devices
    rows, top_count = expert_ids.shape
    outer = devices // 2
    inner_width = local_experts * hidden
    me = lax.axis_index("expert")
    my_group = lax.axis_index("dp")

    def ring(value, step):
        pairs = [(2 * z + x, 2 * ((z + step) % outer) + x) for z in range(outer) for x in range(2)]
        return lax.ppermute(value, "expert", pairs)

    def cross(value):
        return lax.ppermute(value, "expert", [(i, i ^ 1) for i in range(devices)])

    def swap(value, bit):
        return lax.ppermute(value, "dp", [(i, i ^ bit) for i in range(groups)])

    lanes = jnp.arange(LANES, dtype=jnp.int32)
    dense = jnp.sum(
        jnp.where(
            expert_ids[:, :, None] == lanes, route_weights.astype(F32)[:, :, None], 0.0
        ),
        axis=1,
    ).astype(BF)
    grads = jnp.concatenate([out_grad, dense], axis=1)

    gate_up = jnp.concatenate(
        [gate_weight[e] for e in range(local_experts)] + [up_weight[e] for e in range(local_experts)],
        axis=1,
    )
    down_matrix = down_weight.reshape(inner_width, width)

    def middle(linear, grad_rows):
        cotangent = grad_rows[:, :width]
        routes = grad_rows[:, width:].astype(F32)
        weight = jnp.concatenate(
            [
                jnp.broadcast_to(
                    jnp.sum(
                        jnp.where(lanes == me * local_experts + e, routes, 0.0), axis=1, keepdims=True
                    ),
                    (grad_rows.shape[0], hidden),
                )
                for e in range(local_experts)
            ],
            axis=1,
        )
        gate_linear = linear[:, :inner_width]
        up_linear = linear[:, inner_width:]
        delta_hidden = weight * dot(cotangent, down_matrix, 1, 1)
        logistic = jax.nn.sigmoid(gate_linear)
        activated = gate_linear * logistic
        scaled_hidden = (weight * activated * up_linear).astype(BF)
        delta_gate = delta_hidden * up_linear * logistic * (1.0 + gate_linear * (1.0 - logistic))
        delta_up = delta_hidden * activated
        delta = jnp.concatenate([delta_gate.astype(BF), delta_up.astype(BF)], axis=1)
        return delta, scaled_hidden

    def partial_input(delta):
        return dot(delta, gate_up, 1, 1).astype(BF)

    near = my_group
    chunk_order = [near ^ 3, near ^ 2, near ^ 1, near]
    part = width // groups

    def stacked(blocks, axis=0):
        return jnp.concatenate(blocks, axis=axis) if len(blocks) > 1 else blocks[0]

    def by_chunk(blocks):
        return [
            stacked([lax.dynamic_slice(b, (0, c * part), (b.shape[0], part)) for b in blocks]) for c in chunk_order
        ]

    def cotangents(blocks):
        return stacked([g[:, :width] for g in blocks])

    def add(a, b):
        return (a.astype(F32) + b.astype(F32)).astype(BF)

    flying_a = (ring(tokens, 1), cross(tokens))
    flying_b = (ring(grads, 1), cross(grads))
    gate_up = tie(gate_up, grads)[0]
    token_blocks, grad_blocks, deltas, hiddens, own, other = [], [], [], [], [], []
    first_grad_cross = None
    for step in range(1, outer):
        got = tie(*flying_a, *((deltas[-1], hiddens[-1], own[-1], other[-1], first_grad_cross) if own else ()))
        if own:
            deltas[-1], hiddens[-1], own[-1], other[-1], first_grad_cross = got[2:]
        if step == outer - 1:
            flying_a = (cross(got[0]),)
            flying_back = (ring(first_grad_cross, outer - 1),)
        else:
            flying_a = (ring(got[0], 1), cross(got[0]))
        new_tokens = ((tokens,) if step == 1 else ()) + tuple(got[:2])
        token_blocks.append(new_tokens)
        linear = dot(stacked(new_tokens), gate_up, 1, 0)
        got = tie(*flying_b, linear)
        if step == 1:
            first_grad_cross = got[1]
        flying_b = flying_back if step == outer - 1 else (ring(got[0], 1), cross(got[0]))
        new_grads = ((grads,) if step == 1 else ()) + tuple(got[:2])
        grad_blocks.append(new_grads)
        delta, scaled_hidden = middle(got[2], stacked(new_grads))
        deltas.append(delta)
        hiddens.append(scaled_hidden)
        partial = partial_input(delta)
        if step == 1:
            own.append(partial[:rows])
        own.append(partial[-2 * rows : -rows])
        other.append(partial[-rows:])

    early = [t for blocks in token_blocks[:-1] for t in blocks]
    early_delta = stacked(deltas[:-1])
    early_gate_up = [dot(c, early_delta, 0, 0).astype(BF) for c in by_chunk(early)]
    early_down = dot(stacked(hiddens[:-1]), cotangents([g for b in grad_blocks[:-1] for g in b]), 0, 0).astype(BF)
    late_columns = by_chunk(token_blocks[-1])

    last_tokens, *got = tie(*flying_a, *own, *other)
    own, other = got[:outer], got[outer:]
    middle_step = outer // 2
    order = list(range(middle_step, 0, -1)) + list(range(middle_step + 1, outer - 1))
    crossed = {s: cross(other[s]) for s in order}
    late_columns = [stacked([a, b]) for a, b in zip(late_columns, by_chunk([last_tokens]))]
    linear = dot(last_tokens, gate_up, 1, 0)
    got = tie(*flying_b, linear, deltas[-1], hiddens[-1], early_down, *early_gate_up, *late_columns)
    last_grads, linear, deltas[-1], hiddens[-1], early_down = got[:5]
    early_gate_up, late_columns = got[5 : 5 + groups], got[5 + groups :]
    grad_blocks.append((last_grads,))
    load = sum(jnp.sum(g[:, width:].astype(F32), axis=0, keepdims=True) for b in grad_blocks for g in b)
    flying_load = swap(load, 1)
    delta, scaled_hidden = middle(linear, last_grads)
    late_delta = stacked([deltas[-1], delta])
    late_hidden = stacked([hiddens[-1], scaled_hidden])
    late_grads = cotangents([g for b in grad_blocks[-2:] for g in b])

    def whole_chunk(index, late_delta, received=None):
        value = dot(late_columns[index], late_delta, 0, 0) + early_gate_up[index].astype(F32)
        return (value if received is None else value + received.astype(F32)).astype(BF)

    def chunk(index, late_delta, kind, received=None):
        columns = slice(kind * inner_width, (kind + 1) * inner_width)
        value = dot(late_columns[index], late_delta[:, columns], 0, 0) + early_gate_up[index][:, columns].astype(F32)
        return (value if received is None else value + received.astype(F32)).astype(BF)

    def joined(up_part, down_part):
        size = part // 2
        down_part = down_part.reshape(-1, width)
        parts = [v[:, i : i + size] for v in (up_part, down_part) for i in range(0, v.shape[1], size)]
        return jnp.concatenate(parts, axis=0)

    def split(message):
        size = part // 2
        count = inner_width // size
        wide = jnp.concatenate([message[i * part : (i + 1) * part] for i in range(count)], axis=1)
        rest = message[count * part :]
        tall = local_experts * hidden // groups
        narrow = jnp.concatenate([rest[i * tall : (i + 1) * tall] for i in range(width // size)], axis=1)
        return wide, narrow.reshape(local_experts, hidden // groups, width)

    far_gate = chunk(0, late_delta, 0)
    flying_gate = swap(far_gate, 1)
    far_gate, late_delta = tie(far_gate, late_delta)
    far_up = chunk(0, late_delta, 1)
    flying_up = swap(far_up, 1)
    far_up, late_delta, flying_gate, flying_load = tie(far_up, late_delta, flying_gate, flying_load)
    load = load + flying_load
    flying_load = swap(load, 2)
    gate_sum = chunk(1, late_delta, 0, flying_gate)
    flying_gate = swap(gate_sum, 2)
    gate_sum, late_hidden, late_grads, late_delta, value = tie(
        gate_sum, late_hidden, late_grads, late_delta, crossed[middle_step]
    )
    minus = ring(add(own[middle_step], value), outer - 1)
    all_down = (dot(late_hidden, late_grads, 0, 0) + early_down.astype(F32)).astype(BF)
    all_down = all_down.reshape(local_experts, groups, hidden // groups, width)
    down = [lax.dynamic_index_in_dim(all_down, c, 1, keepdims=False) for c in chunk_order]
    flying_down = swap(down[0], 1)
    flying_up, late_delta, delta, *down = tie(flying_up, late_delta, delta, *down)
    up_sum = chunk(1, late_delta, 1, flying_up)
    up_sum, flying_down, delta, late_delta = tie(up_sum, flying_down, delta, late_delta)
    message = joined(up_sum, add(down[1], flying_down))
    flying_far = swap(message, 2)
    message, delta, late_delta, near_down, first_other = tie(message, delta, late_delta, down[2], other[0])
    last_partial = partial_input(delta)
    crossed[outer - 1] = cross(last_partial)
    near_sum = swap(whole_chunk(2, late_delta), 1)
    near_down = swap(near_down, 1)
    crossed[0] = cross(first_other)
    near_sum, near_down, late_delta = tie(near_sum, near_down, late_delta)
    near_sum = whole_chunk(3, late_delta, near_sum)
    near_gate, near_up = near_sum[:, :inner_width], near_sum[:, inner_width:]
    near_down = add(down[3], near_down)
    plus = None
    for s in range(middle_step - 1, 0, -1):
        minus, crossed[s], near_gate, near_up, near_down = tie(minus, crossed[s], near_gate, near_up, near_down)
        minus = ring((own[s].astype(F32) + crossed[s].astype(F32) + minus.astype(F32)).astype(BF), outer - 1)
    for s in range(middle_step + 1, outer):
        if plus is None:
            crossed[s], near_gate = tie(crossed[s], near_gate)
            plus = own[s].astype(F32) + crossed[s].astype(F32)
        else:
            crossed[s], plus, near_gate = tie(crossed[s], plus, near_gate)
            plus = own[s].astype(F32) + crossed[s].astype(F32) + plus.astype(F32)
        plus = ring(plus.astype(BF), 1)

    factor = 1.0 / groups

    def outputs(near, far):
        halves = []
        for e in range(local_experts):
            at = slice(e * hidden, (e + 1) * hidden)
            halves.append(((near[:, at].astype(F32) + far[:, at].astype(F32)) * factor).astype(BF))
        return jnp.stack(halves)

    flying_gate, near_gate = tie(flying_gate, near_gate)
    out_gate = outputs(near_gate, flying_gate)
    minus, plus, crossed[0], out_gate = tie(minus, plus, crossed[0], out_gate)
    grad_input = (
        own[0].astype(F32) + crossed[0].astype(F32) + minus.astype(F32) + plus.astype(F32)
    ).astype(BF)
    flying_far, flying_load, near_up, near_down, grad_input = tie(
        flying_far, flying_load, near_up, near_down, grad_input
    )
    load = load + flying_load
    expert_load = load[0, :num_experts] * (num_experts / (rows * devices * groups * top_count))
    far_up, far_down = split(flying_far)
    out_up = outputs(near_up, far_up)
    out_down = ((near_down.astype(F32) + far_down.astype(F32)) * factor).astype(BF)
    return (grad_input, out_gate, out_up, out_down, expert_load)


def solution(mesh):
    return jax.shard_map(
        shards,
        mesh=mesh,
        in_specs=(
            P(("expert", "dp"), None),
            P(("expert", "dp"), None),
            P(("expert", "dp"), None),
            P(("expert", "dp"), None),
            P("expert", None, None),
            P("expert", None, None),
            P("expert", None, None),
        ),
        out_specs=(
            P(("expert", "dp"), None),
            P("expert", "dp", None),
            P("expert", "dp", None),
            P("expert", "dp", None),
            P(),
        ),
        check_vma=False,
    )
```

```python
import jax
import jax.numpy as jnp
from jax import lax
from jax.sharding import PartitionSpec as P

BF = jnp.bfloat16
F32 = jnp.float32
LANES = 128


def dot(a, b, ca, cb):
    return lax.dot_general(a, b, (((ca,), (cb,)), ((), ())), preferred_element_type=F32)


def tie(*values):
    return lax.optimization_barrier(values)


def shards(tokens, out_grad, route_weights, expert_ids, gate_weight, up_weight, down_weight):
    local_experts, width, hidden = gate_weight.shape
    devices = lax.axis_size("expert")
    groups = lax.axis_size("dp")
    num_experts = local_experts * devices
    rows, top_count = expert_ids.shape
    outer = devices // 2
    inner_width = local_experts * hidden
    me = lax.axis_index("expert")
    my_group = lax.axis_index("dp")

    def ring(value, step):
        pairs = [(2 * z + x, 2 * ((z + step) % outer) + x) for z in range(outer) for x in range(2)]
        return lax.ppermute(value, "expert", pairs)

    def cross(value):
        return lax.ppermute(value, "expert", [(i, i ^ 1) for i in range(devices)])

    def swap(value, bit):
        return lax.ppermute(value, "dp", [(i, i ^ bit) for i in range(groups)])

    lanes = jnp.arange(LANES, dtype=jnp.int32)
    dense = jnp.sum(
        jnp.where(
            expert_ids[:, :, None] == lanes, route_weights.astype(F32)[:, :, None], 0.0
        ),
        axis=1,
    ).astype(BF)
    grads = jnp.concatenate([out_grad, dense], axis=1)

    gate_up = jnp.concatenate(
        [gate_weight[e] for e in range(local_experts)] + [up_weight[e] for e in range(local_experts)],
        axis=1,
    )
    down_matrix = down_weight.reshape(inner_width, width)

    def middle(linear, grad_rows):
        cotangent = grad_rows[:, :width]
        routes = grad_rows[:, width:].astype(F32)
        weight = jnp.concatenate(
            [
                jnp.broadcast_to(
                    jnp.sum(
                        jnp.where(lanes == me * local_experts + e, routes, 0.0), axis=1, keepdims=True
                    ),
                    (grad_rows.shape[0], hidden),
                )
                for e in range(local_experts)
            ],
            axis=1,
        )
        gate_linear = linear[:, :inner_width]
        up_linear = linear[:, inner_width:]
        delta_hidden = weight * dot(cotangent, down_matrix, 1, 1)
        logistic = jax.nn.sigmoid(gate_linear)
        activated = gate_linear * logistic
        scaled_hidden = (weight * activated * up_linear).astype(BF)
        delta_gate = delta_hidden * up_linear * logistic * (1.0 + gate_linear * (1.0 - logistic))
        delta_up = delta_hidden * activated
        delta = jnp.concatenate([delta_gate.astype(BF), delta_up.astype(BF)], axis=1)
        return delta, scaled_hidden

    def partial_input(delta):
        return dot(delta, gate_up, 1, 1).astype(BF)

    near = my_group
    chunk_order = [near ^ 3, near ^ 2, near ^ 1, near]
    part = width // groups

    def stacked(blocks, axis=0):
        return jnp.concatenate(blocks, axis=axis) if len(blocks) > 1 else blocks[0]

    def by_chunk(blocks):
        return [
            stacked([lax.dynamic_slice(b, (0, c * part), (b.shape[0], part)) for b in blocks]) for c in chunk_order
        ]

    def cotangents(blocks):
        return stacked([g[:, :width] for g in blocks])

    def add(a, b):
        return (a.astype(F32) + b.astype(F32)).astype(BF)

    flying_a = (ring(tokens, 1), cross(tokens))
    flying_b = (ring(grads, 1), cross(grads))
    gate_up = tie(gate_up, grads)[0]
    token_blocks, grad_blocks, deltas, hiddens, own, other = [], [], [], [], [], []
    first_grad_cross = None
    for step in range(1, outer):
        got = tie(*flying_a, *((deltas[-1], hiddens[-1], own[-1], other[-1], first_grad_cross) if own else ()))
        if own:
            deltas[-1], hiddens[-1], own[-1], other[-1], first_grad_cross = got[2:]
        if step == outer - 1:
            flying_a = (cross(got[0]),)
            flying_back = (ring(first_grad_cross, outer - 1),)
        else:
            flying_a = (ring(got[0], 1), cross(got[0]))
        new_tokens = ((tokens,) if step == 1 else ()) + tuple(got[:2])
        token_blocks.append(new_tokens)
        linear = dot(stacked(new_tokens), gate_up, 1, 0)
        got = tie(*flying_b, linear)
        if step == 1:
            first_grad_cross = got[1]
        flying_b = flying_back if step == outer - 1 else (ring(got[0], 1), cross(got[0]))
        new_grads = ((grads,) if step == 1 else ()) + tuple(got[:2])
        grad_blocks.append(new_grads)
        delta, scaled_hidden = middle(got[2], stacked(new_grads))
        deltas.append(delta)
        hiddens.append(scaled_hidden)
        partial = partial_input(delta)
        if step == 1:
            own.append(partial[:rows])
        own.append(partial[-2 * rows : -rows])
        other.append(partial[-rows:])

    early = [t for blocks in token_blocks[:-1] for t in blocks]
    early_delta = stacked(deltas[:-1])
    early_gate_up = [dot(c, early_delta, 0, 0).astype(BF) for c in by_chunk(early)]
    early_down = dot(stacked(hiddens[:-1]), cotangents([g for b in grad_blocks[:-1] for g in b]), 0, 0).astype(BF)
    late_columns = by_chunk(token_blocks[-1])

    last_tokens, *got = tie(*flying_a, *own, *other)
    own, other = got[:outer], got[outer:]
    middle_step = outer // 2
    order = list(range(middle_step, 0, -1)) + list(range(middle_step + 1, outer - 1))
    crossed = {s: cross(other[s]) for s in order}
    late_columns = [stacked([a, b]) for a, b in zip(late_columns, by_chunk([last_tokens]))]
    linear = dot(last_tokens, gate_up, 1, 0)
    got = tie(*flying_b, linear, deltas[-1], hiddens[-1], early_down, *early_gate_up, *late_columns)
    last_grads, linear, deltas[-1], hiddens[-1], early_down = got[:5]
    early_gate_up, late_columns = got[5 : 5 + groups], got[5 + groups :]
    grad_blocks.append((last_grads,))
    load = sum(jnp.sum(g[:, width:].astype(F32), axis=0, keepdims=True) for b in grad_blocks for g in b)
    flying_load = swap(load, 1)
    delta, scaled_hidden = middle(linear, last_grads)
    late_delta = stacked([deltas[-1], delta])
    late_hidden = stacked([hiddens[-1], scaled_hidden])
    late_grads = cotangents([g for b in grad_blocks[-2:] for g in b])

    def whole_chunk(index, late_delta, received=None):
        value = dot(late_columns[index], late_delta, 0, 0) + early_gate_up[index].astype(F32)
        return (value if received is None else value + received.astype(F32)).astype(BF)

    def chunk(index, late_delta, kind, received=None):
        columns = slice(kind * inner_width, (kind + 1) * inner_width)
        value = dot(late_columns[index], late_delta[:, columns], 0, 0) + early_gate_up[index][:, columns].astype(F32)
        return (value if received is None else value + received.astype(F32)).astype(BF)

    def joined(up_part, down_part):
        size = part // 2
        down_part = down_part.reshape(-1, width)
        parts = [v[:, i : i + size] for v in (up_part, down_part) for i in range(0, v.shape[1], size)]
        return jnp.concatenate(parts, axis=0)

    def split(message):
        size = part // 2
        count = inner_width // size
        wide = jnp.concatenate([message[i * part : (i + 1) * part] for i in range(count)], axis=1)
        rest = message[count * part :]
        tall = local_experts * hidden // groups
        narrow = jnp.concatenate([rest[i * tall : (i + 1) * tall] for i in range(width // size)], axis=1)
        return wide, narrow.reshape(local_experts, hidden // groups, width)

    far_gate = chunk(0, late_delta, 0)
    flying_gate = swap(far_gate, 1)
    far_gate, late_delta = tie(far_gate, late_delta)
    far_up = chunk(0, late_delta, 1)
    flying_up = swap(far_up, 1)
    all_down = (dot(late_hidden, late_grads, 0, 0) + early_down.astype(F32)).astype(BF)
    far_up, late_delta, flying_gate, all_down = tie(far_up, late_delta, flying_gate, all_down)
    gate_sum = chunk(1, late_delta, 0, flying_gate)
    flying_gate = swap(gate_sum, 2)
    gate_sum, late_hidden, late_grads, late_delta, value = tie(
        gate_sum, late_hidden, late_grads, late_delta, crossed[middle_step]
    )
    minus = ring(add(own[middle_step], value), outer - 1)
    all_down = all_down.reshape(local_experts, groups, hidden // groups, width)
    down = [lax.dynamic_index_in_dim(all_down, c, 1, keepdims=False) for c in chunk_order]
    flying_down = swap(down[0], 1)
    flying_up, late_delta, delta, *down = tie(flying_up, late_delta, delta, *down)
    up_sum = chunk(1, late_delta, 1, flying_up)
    up_sum, flying_down, delta, late_delta = tie(up_sum, flying_down, delta, late_delta)
    message = joined(up_sum, add(down[1], flying_down))
    flying_far = swap(message, 2)
    message, delta, late_delta, near_down, first_other, flying_load = tie(
        message, delta, late_delta, down[2], other[0], flying_load
    )
    load = load + flying_load
    flying_load = swap(load, 2)
    last_partial = partial_input(delta)
    crossed[outer - 1] = cross(last_partial)
    near_sum = swap(whole_chunk(2, late_delta), 1)
    near_down = swap(near_down, 1)
    crossed[0] = cross(first_other)
    near_sum, near_down, late_delta = tie(near_sum, near_down, late_delta)
    near_sum = whole_chunk(3, late_delta, near_sum)
    near_gate, near_up = near_sum[:, :inner_width], near_sum[:, inner_width:]
    near_down = add(down[3], near_down)
    plus = None
    for s in range(middle_step - 1, 0, -1):
        minus, crossed[s], near_gate, near_up, near_down = tie(minus, crossed[s], near_gate, near_up, near_down)
        minus = ring((own[s].astype(F32) + crossed[s].astype(F32) + minus.astype(F32)).astype(BF), outer - 1)
    for s in range(middle_step + 1, outer):
        if plus is None:
            crossed[s], near_gate = tie(crossed[s], near_gate)
            plus = own[s].astype(F32) + crossed[s].astype(F32)
        else:
            crossed[s], plus, near_gate = tie(crossed[s], plus, near_gate)
            plus = own[s].astype(F32) + crossed[s].astype(F32) + plus.astype(F32)
        plus = ring(plus.astype(BF), 1)

    factor = 1.0 / groups

    def outputs(near, far):
        halves = []
        for e in range(local_experts):
            at = slice(e * hidden, (e + 1) * hidden)
            halves.append(((near[:, at].astype(F32) + far[:, at].astype(F32)) * factor).astype(BF))
        return jnp.stack(halves)

    flying_gate, near_gate = tie(flying_gate, near_gate)
    out_gate = outputs(near_gate, flying_gate)
    minus, plus, crossed[0], out_gate = tie(minus, plus, crossed[0], out_gate)
    grad_input = (
        own[0].astype(F32) + crossed[0].astype(F32) + minus.astype(F32) + plus.astype(F32)
    ).astype(BF)
    flying_far, flying_load, near_up, near_down, grad_input = tie(
        flying_far, flying_load, near_up, near_down, grad_input
    )
    load = load + flying_load
    expert_load = load[0, :num_experts] * (num_experts / (rows * devices * groups * top_count))
    far_up, far_down = split(flying_far)
    out_up = outputs(near_up, far_up)
    out_down = ((near_down.astype(F32) + far_down.astype(F32)) * factor).astype(BF)
    return (grad_input, out_gate, out_up, out_down, expert_load)


def solution(mesh):
    return jax.shard_map(
        shards,
        mesh=mesh,
        in_specs=(
            P(("expert", "dp"), None),
            P(("expert", "dp"), None),
            P(("expert", "dp"), None),
            P(("expert", "dp"), None),
            P("expert", None, None),
            P("expert", None, None),
            P("expert", None, None),
        ),
        out_specs=(
            P(("expert", "dp"), None),
            P("expert", "dp", None),
            P("expert", "dp", None),
            P("expert", "dp", None),
            P(),
        ),
        check_vma=False,
    )
```

```python
import jax
import jax.numpy as jnp
from jax import lax
from jax.sharding import PartitionSpec as P

BF = jnp.bfloat16
F32 = jnp.float32
LANES = 128


def dot(a, b, ca, cb):
    return lax.dot_general(a, b, (((ca,), (cb,)), ((), ())), preferred_element_type=F32)


def tie(*values):
    return lax.optimization_barrier(values)


def shards(tokens, out_grad, route_weights, expert_ids, gate_weight, up_weight, down_weight):
    local_experts, width, hidden = gate_weight.shape
    devices = lax.axis_size("expert")
    groups = lax.axis_size("dp")
    num_experts = local_experts * devices
    rows, top_count = expert_ids.shape
    outer = devices // 2
    inner_width = local_experts * hidden
    me = lax.axis_index("expert")
    my_group = lax.axis_index("dp")

    def ring(value, step):
        pairs = [(2 * z + x, 2 * ((z + step) % outer) + x) for z in range(outer) for x in range(2)]
        return lax.ppermute(value, "expert", pairs)

    def cross(value):
        return lax.ppermute(value, "expert", [(i, i ^ 1) for i in range(devices)])

    def swap(value, bit):
        return lax.ppermute(value, "dp", [(i, i ^ bit) for i in range(groups)])

    lanes = jnp.arange(LANES, dtype=jnp.int32)
    dense = jnp.sum(
        jnp.where(
            expert_ids[:, :, None] == lanes, route_weights.astype(F32)[:, :, None], 0.0
        ),
        axis=1,
    ).astype(BF)
    grads = jnp.concatenate([out_grad, dense], axis=1)

    gate_up = jnp.concatenate(
        [gate_weight[e] for e in range(local_experts)] + [up_weight[e] for e in range(local_experts)],
        axis=1,
    )
    down_matrix = down_weight.reshape(inner_width, width)

    def middle(linear, grad_rows):
        cotangent = grad_rows[:, :width]
        routes = grad_rows[:, width:].astype(F32)
        weight = jnp.concatenate(
            [
                jnp.broadcast_to(
                    jnp.sum(
                        jnp.where(lanes == me * local_experts + e, routes, 0.0), axis=1, keepdims=True
                    ),
                    (grad_rows.shape[0], hidden),
                )
                for e in range(local_experts)
            ],
            axis=1,
        )
        gate_linear = linear[:, :inner_width]
        up_linear = linear[:, inner_width:]
        delta_hidden = weight * dot(cotangent, down_matrix, 1, 1)
        logistic = jax.nn.sigmoid(gate_linear)
        activated = gate_linear * logistic
        scaled_hidden = (weight * activated * up_linear).astype(BF)
        delta_gate = delta_hidden * up_linear * logistic * (1.0 + gate_linear * (1.0 - logistic))
        delta_up = delta_hidden * activated
        delta = jnp.concatenate([delta_gate.astype(BF), delta_up.astype(BF)], axis=1)
        return delta, scaled_hidden

    def partial_input(delta):
        return dot(delta, gate_up, 1, 1).astype(BF)

    near = my_group
    chunk_order = [near ^ 3, near ^ 2, near ^ 1, near]
    part = width // groups

    def stacked(blocks, axis=0):
        return jnp.concatenate(blocks, axis=axis) if len(blocks) > 1 else blocks[0]

    def by_chunk(blocks):
        return [
            stacked([lax.dynamic_slice(b, (0, c * part), (b.shape[0], part)) for b in blocks]) for c in chunk_order
        ]

    def cotangents(blocks):
        return stacked([g[:, :width] for g in blocks])

    def add(a, b):
        return (a.astype(F32) + b.astype(F32)).astype(BF)

    flying_a = (ring(tokens, 1), cross(tokens))
    flying_b = (ring(grads, 1), cross(grads))
    gate_up = tie(gate_up, grads)[0]
    token_blocks, grad_blocks, deltas, hiddens, own, other = [], [], [], [], [], []
    first_grad_cross = None
    for step in range(1, outer):
        got = tie(*flying_a, *((deltas[-1], hiddens[-1], own[-1], other[-1], first_grad_cross) if own else ()))
        if own:
            deltas[-1], hiddens[-1], own[-1], other[-1], first_grad_cross = got[2:]
        if step == outer - 1:
            flying_a = (cross(got[0]),)
            flying_back = (ring(first_grad_cross, outer - 1),)
        else:
            flying_a = (ring(got[0], 1), cross(got[0]))
        new_tokens = ((tokens,) if step == 1 else ()) + tuple(got[:2])
        token_blocks.append(new_tokens)
        linear = dot(stacked(new_tokens), gate_up, 1, 0)
        got = tie(*flying_b, linear)
        if step == 1:
            first_grad_cross = got[1]
        flying_b = flying_back if step == outer - 1 else (ring(got[0], 1), cross(got[0]))
        new_grads = ((grads,) if step == 1 else ()) + tuple(got[:2])
        grad_blocks.append(new_grads)
        delta, scaled_hidden = middle(got[2], stacked(new_grads))
        deltas.append(delta)
        hiddens.append(scaled_hidden)
        partial = partial_input(delta)
        if step == 1:
            own.append(partial[:rows])
        own.append(partial[-2 * rows : -rows])
        other.append(partial[-rows:])

    early = [t for blocks in token_blocks[:-1] for t in blocks]
    early_delta = stacked(deltas[:-1])
    early_gate_up = [dot(c, early_delta, 0, 0).astype(BF) for c in by_chunk(early)]
    early_down = dot(stacked(hiddens[:-1]), cotangents([g for b in grad_blocks[:-1] for g in b]), 0, 0).astype(BF)
    late_columns = by_chunk(token_blocks[-1])

    last_tokens, *got = tie(*flying_a, *own, *other)
    own, other = got[:outer], got[outer:]
    middle_step = outer // 2
    order = list(range(middle_step, 0, -1)) + list(range(middle_step + 1, outer - 1))
    crossed = {s: cross(other[s]) for s in order}
    late_columns = [stacked([a, b]) for a, b in zip(late_columns, by_chunk([last_tokens]))]
    linear = dot(last_tokens, gate_up, 1, 0)
    got = tie(*flying_b, linear, deltas[-1], hiddens[-1], early_down, *early_gate_up, *late_columns)
    last_grads, linear, deltas[-1], hiddens[-1], early_down = got[:5]
    early_gate_up, late_columns = got[5 : 5 + groups], got[5 + groups :]
    grad_blocks.append((last_grads,))
    load = sum(jnp.sum(g[:, width:].astype(F32), axis=0, keepdims=True) for b in grad_blocks for g in b)
    flying_load = swap(load, 1)
    delta, scaled_hidden = middle(linear, last_grads)
    late_delta = stacked([deltas[-1], delta])
    late_hidden = stacked([hiddens[-1], scaled_hidden])
    late_grads = cotangents([g for b in grad_blocks[-2:] for g in b])

    def whole_chunk(index, late_delta, received=None):
        value = dot(late_columns[index], late_delta, 0, 0) + early_gate_up[index].astype(F32)
        return (value if received is None else value + received.astype(F32)).astype(BF)

    def chunk(index, late_delta, kind, received=None):
        columns = slice(kind * inner_width, (kind + 1) * inner_width)
        value = dot(late_columns[index], late_delta[:, columns], 0, 0) + early_gate_up[index][:, columns].astype(F32)
        return (value if received is None else value + received.astype(F32)).astype(BF)

    def joined(up_part, down_part):
        size = part // 2
        down_part = down_part.reshape(-1, width)
        parts = [v[:, i : i + size] for v in (up_part, down_part) for i in range(0, v.shape[1], size)]
        return jnp.concatenate(parts, axis=0)

    def split(message):
        size = part // 2
        count = inner_width // size
        wide = jnp.concatenate([message[i * part : (i + 1) * part] for i in range(count)], axis=1)
        rest = message[count * part :]
        tall = local_experts * hidden // groups
        narrow = jnp.concatenate([rest[i * tall : (i + 1) * tall] for i in range(width // size)], axis=1)
        return wide, narrow.reshape(local_experts, hidden // groups, width)

    far_gate = chunk(0, late_delta, 0)
    flying_gate = swap(far_gate, 1)
    far_gate, late_delta = tie(far_gate, late_delta)
    far_up = chunk(0, late_delta, 1)
    flying_up = swap(far_up, 1)
    all_down = (dot(late_hidden, late_grads, 0, 0) + early_down.astype(F32)).astype(BF)
    far_up, late_delta, flying_gate, all_down = tie(far_up, late_delta, flying_gate, all_down)
    gate_sum = chunk(1, late_delta, 0, flying_gate)
    flying_gate = swap(gate_sum, 2)
    gate_sum, value = tie(gate_sum, crossed[middle_step])
    minus = ring(add(own[middle_step], value), outer - 1)
    all_down = all_down.reshape(local_experts, groups, hidden // groups, width)
    down = [lax.dynamic_index_in_dim(all_down, c, 1, keepdims=False) for c in chunk_order]
    flying_down = swap(down[0], 1)
    flying_up, late_delta, delta, *down = tie(flying_up, late_delta, delta, *down)
    up_sum = chunk(1, late_delta, 1, flying_up)
    up_sum, flying_down, delta, late_delta = tie(up_sum, flying_down, delta, late_delta)
    message = joined(up_sum, add(down[1], flying_down))
    flying_far = swap(message, 2)
    message, delta, late_delta, near_down, first_other, flying_load = tie(
        message, delta, late_delta, down[2], other[0], flying_load
    )
    load = load + flying_load
    flying_load = swap(load, 2)
    last_partial = partial_input(delta)
    crossed[outer - 1] = cross(last_partial)
    near_sum = swap(whole_chunk(2, late_delta), 1)
    near_down = swap(near_down, 1)
    crossed[0] = cross(first_other)
    near_sum, near_down, late_delta = tie(near_sum, near_down, late_delta)
    near_sum = whole_chunk(3, late_delta, near_sum)
    near_gate, near_up = near_sum[:, :inner_width], near_sum[:, inner_width:]
    near_down = add(down[3], near_down)
    plus = None
    for s in range(middle_step - 1, 0, -1):
        minus, crossed[s], near_gate, near_up, near_down = tie(minus, crossed[s], near_gate, near_up, near_down)
        minus = ring((own[s].astype(F32) + crossed[s].astype(F32) + minus.astype(F32)).astype(BF), outer - 1)
    for s in range(middle_step + 1, outer):
        if plus is None:
            crossed[s], near_gate = tie(crossed[s], near_gate)
            plus = own[s].astype(F32) + crossed[s].astype(F32)
        else:
            crossed[s], plus, near_gate = tie(crossed[s], plus, near_gate)
            plus = own[s].astype(F32) + crossed[s].astype(F32) + plus.astype(F32)
        plus = ring(plus.astype(BF), 1)

    factor = 1.0 / groups

    def outputs(near, far):
        halves = []
        for e in range(local_experts):
            at = slice(e * hidden, (e + 1) * hidden)
            halves.append(((near[:, at].astype(F32) + far[:, at].astype(F32)) * factor).astype(BF))
        return jnp.stack(halves)

    flying_gate, near_gate = tie(flying_gate, near_gate)
    out_gate = outputs(near_gate, flying_gate)
    minus, plus, crossed[0], out_gate = tie(minus, plus, crossed[0], out_gate)
    grad_input = (
        own[0].astype(F32) + crossed[0].astype(F32) + minus.astype(F32) + plus.astype(F32)
    ).astype(BF)
    flying_far, flying_load, near_up, near_down, grad_input = tie(
        flying_far, flying_load, near_up, near_down, grad_input
    )
    load = load + flying_load
    expert_load = load[0, :num_experts] * (num_experts / (rows * devices * groups * top_count))
    far_up, far_down = split(flying_far)
    out_up = outputs(near_up, far_up)
    out_down = ((near_down.astype(F32) + far_down.astype(F32)) * factor).astype(BF)
    return (grad_input, out_gate, out_up, out_down, expert_load)


def solution(mesh):
    return jax.shard_map(
        shards,
        mesh=mesh,
        in_specs=(
            P(("expert", "dp"), None),
            P(("expert", "dp"), None),
            P(("expert", "dp"), None),
            P(("expert", "dp"), None),
            P("expert", None, None),
            P("expert", None, None),
            P("expert", None, None),
        ),
        out_specs=(
            P(("expert", "dp"), None),
            P("expert", "dp", None),
            P("expert", "dp", None),
            P("expert", "dp", None),
            P(),
        ),
        check_vma=False,
    )
```
